1024 devices in a mesh: dp: 128 (over x_lo, y, z), expert: 8 (over x_hi, core).
Axes of the slice: x: 8 (x_hi: 4, x_lo: 2; x = x_hi * 2 + x_lo), y: 8, z: 8, core: 2. Of those that a mesh axis runs over, the one named last changes fastest.
Arguments:
- cotangent: bfloat16 [131072, 4096], P(('dp', 'expert')), may hold values from -6 to 6
- gate_up: bfloat16 [131072, 1, 1536], P(('dp', 'expert')), may hold values from -6 to 6
- route_probs: bfloat16 [131072, 1], P(('dp', 'expert')), may hold values from 0.049804688 to 0.59765625
- routes: int32 [131072, 1], P(('dp', 'expert')), may hold values from 0 to 7; in each aligned block of 128 rows (0 to 127, 128 to 255, ...) at most 20 rows name the same one
- down_weight: bfloat16 [8, 4096, 768], P('expert', 'dp'), may hold values from -0.09375 to 0.09375
Outputs:
- grad_gate_up: bfloat16 [131072, 1, 1536], P(('dp', 'expert'))
- grad_probs: bfloat16 [131072, 1], P(('dp', 'expert'))
The draws below stay inside these ranges and needn't reach their ends.
Inputs may be any that keep to these rules, and one draw needn't show every extreme that they name: `routes`: each token names exactly one expert; among the 128 tokens of one device no expert is named by more than 20 tokens, and on some device some expert is named by exactly 20.
All inputs are finite; a program needn't handle non-finite values.
Results may differ from the reference program's by a relative error of at most 0.015.
Values may be sent and summed in bfloat16 or wider, within the bound.
No kernel may reach another device: no remote copies, remote signals or barrier semaphores. Data moves between devices by JAX's collectives and lax.ppermute only.
A program may use at most 32 MiB of HBM per device.

```python
import math
import jax
import jax.numpy as jnp
import numpy as np
from jax import lax

D = 4096
FFW = 768
TOP_WIN = 1
TOK_DEV = 128
CAP = 20
EXPERTS = 8
TOKENS = 131072


def level_of(own_key, dims, pieces, smallest, largest):
    gain = 1.0
    for axis_at, parts in pieces:
        steps = jax.random.uniform(jax.random.fold_in(jax.random.fold_in(own_key, 6), axis_at), (parts,), jnp.float32, smallest / len(pieces), largest / len(pieces))
        gain = gain * jnp.repeat(jnp.exp(steps), dims[axis_at] // parts).reshape((-1,) + (1,) * (len(dims) - 1 - axis_at))
    return gain


def routed_block(own_key, own, number, rows, amount, top, reach, lean):
    sequence = jax.random.permutation(own_key, amount)
    crowded, common = shares(amount, rows * top, reach, lean, True), shares(amount, rows * top, reach, lean, False)
    places = jnp.arange(amount)

    def named(lengths, turn):
        used = int((lengths > 0).sum())
        fixed = max(1, used // 4)
        moved = fixed + (places - fixed + turn * (used - fixed)) % max(1, amount - fixed)
        return jnp.zeros((amount,), jnp.int32).at[sequence[jnp.where(places < fixed, places, moved)]].set(jnp.asarray(lengths, jnp.int32))

    lengths = jnp.where(number % 4 == 0, named(crowded, number // 4), named(common, number - number // 4 - 1))
    mixed = jax.random.permutation(jax.random.fold_in(own, 3), amount)
    source_of, receiver = mixed[0:amount // 2 * 2:2], mixed[1:amount // 2 * 2:2]
    room = jnp.minimum(lengths[source_of] - 1, reach - lengths[receiver]) // 2
    room = jnp.where((source_of == sequence[0]) | (receiver == sequence[0]) | (lengths[receiver] == 0), 0, jnp.maximum(room, 0))
    moved = jax.random.randint(jax.random.fold_in(own, 4), (amount // 2,), 0, 1 << 20) % (room + 1)
    lengths = lengths.at[source_of].add(-moved).at[receiver].add(moved)
    items = jnp.searchsorted(jnp.cumsum(lengths), jnp.arange(rows * top), side="right").astype(jnp.int32)
    listing = items.reshape(top, rows).T
    listing = listing[jax.random.permutation(jax.random.fold_in(own, 1), rows)]
    turn = jax.random.randint(jax.random.fold_in(own, 2), (rows, 1), 0, top)
    return jnp.take_along_axis(listing, (jnp.arange(top)[None, :] + turn) % top, axis=1)


def shares(number_of, total, most, lean, full):
    weights = [(1 << 20) // math.isqrt(grade ** lean) + 1 for grade in range(1, number_of + 1)]
    largest = most if full else min(most, max(-(-total // number_of), total * weights[0] // sum(weights)))
    least = 1 if total - largest >= number_of - 1 else 0
    holding, spare = [largest] + [least] * (number_of - 1), total - largest - least * (number_of - 1)
    while spare > 0:
        movable = [i for i in range(1, number_of) if holding[i] < largest] or [i for i in range(1, number_of) if holding[i] < most]
        whole, remaining = sum([weights[i] for i in movable]), spare
        for i in movable:
            addition = min(most - holding[i], max(1, remaining * weights[i] // whole), spare)
            holding[i] = holding[i] + addition
            spare = spare - addition
    return np.array(holding)


def normal_values(stream_key, shape, scale, limit, pieces=(), kind=jnp.bfloat16):
    loudness = level_of(stream_key, shape, pieces, -0.22, 0.18) if pieces else 1.0
    array = jax.random.normal(stream_key, shape, jnp.float32) * scale * loudness
    return jnp.minimum(jnp.maximum(array, -limit), limit).astype(kind)


def setup_inputs(seed: int = 0) -> dict:
    key_list = jax.random.split(jax.random.key(seed), 6)
    cotangent = normal_values(key_list[0], (TOKENS, D), 1.0, 6.0, ((0, 1024),))
    gate_up = normal_values(key_list[1], (TOKENS, TOP_WIN, 2 * FFW), 1.0, 6.0, ((0, 1024),))
    route_probs = jnp.clip(jnp.exp(math.log(0.59765625) - 2.4849066 * jax.random.uniform(key_list[2], (TOKENS, TOP_WIN), jnp.float32) ** level_of(key_list[2], (TOKENS, TOP_WIN), ((0, 1024),), -0.2, 0.2)), 0.049804688, 0.59765625).astype(jnp.bfloat16)
    routes_keys = jax.random.split(jax.random.fold_in(key_list[3], 1), TOKENS // TOK_DEV)
    routes_turns = jax.random.permutation(jax.random.fold_in(key_list[3], 3), TOKENS // TOK_DEV)
    routes = jax.vmap(lambda own, number: routed_block(jax.random.fold_in(key_list[3], 2), own, number, TOK_DEV, EXPERTS, TOP_WIN, CAP, 2))(routes_keys, routes_turns).reshape((TOKENS, TOP_WIN))
    down_weight = normal_values(key_list[4], (EXPERTS, D, FFW), D ** -0.5, 0.09375, ((0, 8), (1, 128)))
    return dict(cotangent=cotangent, gate_up=gate_up, route_probs=route_probs, routes=routes, down_weight=down_weight)


row_block = 512


def reference(cotangent, gate_up, route_probs, routes, down_weight):
    route_rows = TOKENS * TOP_WIN
    flat_routes = routes.reshape(route_rows).astype(jnp.int32)
    sorted_order = jnp.argsort(flat_routes, stable=True).astype(jnp.int32)
    labels = jnp.arange(EXPERTS, dtype=jnp.int32)
    counts = jnp.sum((flat_routes[:, None] == labels[None, :]).astype(jnp.int32), axis=0).astype(jnp.int32)
    starts = (jnp.cumsum(counts) - counts).astype(jnp.int32)
    padded = (((counts + row_block - 1) // row_block) * row_block).astype(jnp.int32)
    pad_starts = (jnp.cumsum(padded) - padded).astype(jnp.int32)
    pad_ends = (pad_starts + padded).astype(jnp.int32)
    sorted_ids = flat_routes[sorted_order]
    within = (jnp.arange(route_rows, dtype=jnp.int32) - starts[sorted_ids]).astype(jnp.int32)
    slot_dest = (pad_starts[sorted_ids] + within).astype(jnp.int32)
    block_count = route_rows // row_block + 1 + EXPERTS
    padded_total = block_count * row_block
    source = jnp.zeros((padded_total,), jnp.int32).at[slot_dest].set((sorted_order // TOP_WIN).astype(jnp.int32))
    row_slot = jnp.zeros((route_rows,), jnp.int32).at[sorted_order].set(slot_dest)
    block_first = jnp.arange(block_count, dtype=jnp.int32) * row_block
    block_expert = jnp.minimum(jnp.sum((pad_ends[None, :] <= block_first[:, None]).astype(jnp.int32), axis=1), EXPERTS - 1).astype(jnp.int32)

    def one_block(block_index):
        block_tokens = lax.dynamic_slice_in_dim(source, block_index * row_block, row_block)
        block_rows = cotangent[block_tokens]
        weight = down_weight[block_expert[block_index]]
        return jnp.dot(block_rows, weight, preferred_element_type=jnp.float32)

    back_padded = lax.map(one_block, jnp.arange(block_count, dtype=jnp.int32))
    back_hidden = back_padded.reshape(padded_total, FFW)[row_slot].reshape(TOKENS, TOP_WIN, FFW)
    gate_pre = gate_up[..., :FFW].astype(jnp.float32)
    up_value = gate_up[..., FFW:].astype(jnp.float32)
    squash = jax.nn.sigmoid(gate_pre)
    hidden = (gate_pre * squash * up_value).astype(jnp.bfloat16)
    grad_probs = jnp.sum(hidden.astype(jnp.float32) * back_hidden, axis=-1).astype(jnp.bfloat16)
    scaled = route_probs.astype(jnp.float32)[..., None] * back_hidden
    grad_gate = scaled * up_value * squash * (1.0 + gate_pre * (1.0 - squash))
    grad_up = scaled * gate_pre * squash
    grad_gate_up = jnp.concatenate([grad_gate, grad_up], axis=-1).astype(jnp.bfloat16)
    return grad_gate_up, grad_probs
```

```python
import jax
import jax.numpy as jnp
from jax import lax
from jax.sharding import Mesh, PartitionSpec as P

D = 4096
FFW = 768

AXES = ("xl", "y", "z", "xh", "core")
EXPERT = ("xh", "core")


def body(cotangent, gate_up, route_probs, routes, down_weight):
    tokens = cotangent.shape[0]
    groups = 8
    capacity = tokens // groups + tokens // 32
    slot_count = groups * capacity

    pair = lax.all_gather(down_weight[0], "xl", axis=0, tiled=False)
    weight = lax.all_gather(pair, ("y", "z"), axis=1, tiled=True).reshape(D, FFW)

    flat_routes = routes.reshape(tokens)
    member = (flat_routes[:, None] == jnp.arange(groups, dtype=jnp.int32)[None, :]).astype(jnp.int32)
    rank = jnp.sum(jnp.cumsum(member, axis=0) * member, axis=1) - 1
    target = flat_routes * capacity + rank
    placing = (jnp.arange(slot_count, dtype=jnp.int32)[:, None] == target[None, :]).astype(jnp.bfloat16)

    rows_cot = (
        jnp.dot(placing, cotangent, preferred_element_type=jnp.float32)
        .astype(jnp.bfloat16)
        .reshape(groups, capacity, D)
    )
    slot_rows = lax.all_to_all(rows_cot, EXPERT, split_axis=0, concat_axis=0, tiled=True)

    back = jnp.dot(slot_rows.reshape(slot_count, D), weight, preferred_element_type=jnp.float32)
    back = back.astype(jnp.bfloat16).reshape(groups, capacity, FFW)
    came = lax.all_to_all(back, EXPERT, split_axis=0, concat_axis=0, tiled=True)
    back_hidden = lax.dot_general(
        placing,
        came.reshape(slot_count, FFW),
        (((0,), (0,)), ((), ())),
        preferred_element_type=jnp.float32,
    )

    flat_pre = gate_up.reshape(tokens, 2 * FFW)
    gate = flat_pre[:, :FFW].astype(jnp.float32)
    up = flat_pre[:, FFW:].astype(jnp.float32)
    squash = jax.nn.sigmoid(gate)
    hidden = (gate * squash * up).astype(jnp.bfloat16).astype(jnp.float32)
    grad_probs = jnp.sum(hidden * back_hidden, axis=1, keepdims=True).astype(jnp.bfloat16)
    scaled = route_probs.astype(jnp.float32) * back_hidden
    grad_gate = scaled * up * squash * (1.0 + gate * (1.0 - squash))
    grad_up = scaled * gate * squash
    grads = jnp.concatenate([grad_gate, grad_up], axis=-1).astype(jnp.bfloat16)
    return grads.reshape(tokens, 1, 2 * FFW), grad_probs


def solution(mesh):
    named = Mesh(mesh.devices.reshape(2, 8, 8, 4, 2), AXES)
    dp = ("xl", "y", "z")
    return jax.shard_map(
        body,
        mesh=named,
        in_specs=(
            P(AXES, None),
            P(AXES, None, None),
            P(AXES, None),
            P(AXES, None),
            P(EXPERT, dp, None),
        ),
        out_specs=(P(AXES, None, None), P(AXES, None)),
        check_vma=False,
    )
```

```python
import jax
import jax.numpy as jnp
from jax import lax
from jax.sharding import Mesh, PartitionSpec as P

D = 4096
FFW = 768
HALF = D // 2
QUART = D // 4
EXPERTS = 8
CAP = 20
PEERS = 16

AXES = ("xl", "y", "z", "xh", "core")
SHARE = ("xl", "xh", "core")


def onehot(index, rows):
    return (jnp.arange(rows, dtype=jnp.int32)[:, None] == index[None, :]).astype(jnp.bfloat16)


def body(cotangent, gate_up, route_probs, routes, down_weight):
    tokens = cotangent.shape[0]

    weight = lax.all_gather(down_weight[0], ("y", "z"), axis=0, tiled=True)

    flat_routes = routes.reshape(tokens)
    member = (flat_routes[:, None] == jnp.arange(EXPERTS, dtype=jnp.int32)[None, :]).astype(jnp.int32)
    rank = jnp.sum(jnp.cumsum(member, axis=0) * member, axis=1) - 1
    first = flat_routes * (2 * CAP) + rank
    both = jnp.concatenate([first, first + CAP])
    placing = onehot(both, EXPERTS * 2 * CAP)
    quarters = [cotangent[:, i * QUART : (i + 1) * QUART] for i in range(4)]
    sent = jnp.stack(
        [
            jnp.dot(
                placing,
                jnp.concatenate([quarters[2 * h], quarters[2 * h + 1]], axis=0),
                preferred_element_type=jnp.float32,
            ).astype(jnp.bfloat16)
            for h in range(2)
        ]
    ).reshape(PEERS, 2 * CAP, QUART)
    got = lax.all_to_all(sent, SHARE, split_axis=0, concat_axis=0, tiled=True)

    count = PEERS * 2 * CAP
    order = jnp.arange(count, dtype=jnp.int32)
    order = (order % (count // 2)) // CAP * (2 * CAP) + order // (count // 2) * CAP + order % CAP
    swap = onehot(order, count)
    rows = lax.dot_general(
        swap, got.reshape(count, QUART), (((0,), (0,)), ((), ())), preferred_element_type=jnp.float32
    ).astype(jnp.bfloat16)
    back = jnp.dot(rows[: count // 2], weight[:QUART], preferred_element_type=jnp.float32) + jnp.dot(
        rows[count // 2 :], weight[QUART:], preferred_element_type=jnp.float32
    )
    back = back.astype(jnp.bfloat16)
    back = jnp.concatenate([back[:, : FFW // 2], back[:, FFW // 2 :]], axis=0)
    back = jnp.dot(swap, back, preferred_element_type=jnp.float32).astype(jnp.bfloat16)
    came = lax.all_to_all(
        back.reshape(PEERS, 2 * CAP, FFW // 2), SHARE, split_axis=0, concat_axis=0, tiled=True
    ).reshape(count, FFW // 2)

    place = jnp.arange(count, dtype=jnp.int32) % (count // 2)
    back_hidden = jnp.concatenate(
        [
            jnp.dot(
                (place[None, :] == (first + c * CAP)[:, None]).astype(jnp.bfloat16),
                came,
                preferred_element_type=jnp.float32,
            )
            for c in range(2)
        ],
        axis=1,
    )

    flat_pre = gate_up.reshape(tokens, 2 * FFW)
    gate = flat_pre[:, :FFW].astype(jnp.float32)
    up = flat_pre[:, FFW:].astype(jnp.float32)
    squash = jax.nn.sigmoid(gate)
    hidden = (gate * squash * up).astype(jnp.bfloat16).astype(jnp.float32)
    grad_probs = jnp.sum(hidden * back_hidden, axis=1, keepdims=True).astype(jnp.bfloat16)
    scaled = route_probs.astype(jnp.float32) * back_hidden
    grad_gate = scaled * up * squash * (1.0 + gate * (1.0 - squash))
    grad_up = scaled * gate * squash
    grads = jnp.concatenate([grad_gate, grad_up], axis=-1).astype(jnp.bfloat16)
    return grads.reshape(tokens, 1, 2 * FFW), grad_probs


def solution(mesh):
    named = Mesh(mesh.devices.reshape(2, 8, 8, 4, 2), AXES)
    return jax.shard_map(
        body,
        mesh=named,
        in_specs=(
            P(AXES, None),
            P(AXES, None, None),
            P(AXES, None),
            P(AXES, None),
            P(("xh", "core"), ("xl", "y", "z"), None),
        ),
        out_specs=(P(AXES, None, None), P(AXES, None)),
        check_vma=False,
    )
```

```python
import jax
import jax.numpy as jnp
from jax import lax
from jax.experimental import pallas as pl
from jax.experimental.pallas import tpu as pltpu
from jax.sharding import Mesh, PartitionSpec as P

D = 4096
FFW = 768
HALF = D // 2
QUART = D // 4
EXPERTS = 8
CAP = 20
PEERS = 16

AXES = ("xl", "y", "z", "xh", "core")
SHARE = ("xl", "xh", "core")

TORUS = ("y", "z", "xh", "core")
RING = 8
LINES = [(h, c) for h in range(4) for c in range(2)]
COUNT = PEERS * 2 * CAP


def place_of(y, z, h, c):
    return (((y % RING) * RING + z % RING) * 4 + h) * 2 + c


def first_groups():
    return [
        [place_of(k, i, h, c) if c == 0 else place_of(i, k, h, c) for i in range(RING)]
        for h, c in LINES
        for k in range(RING)
    ]


def second_shift(step):
    return [
        (place_of(y, z, h, c), place_of(y + step, z, h, c) if c == 0 else place_of(y, z + step, h, c))
        for y in range(RING)
        for z in range(RING)
        for h, c in LINES
    ]


def product(got_ref, *refs):
    parts, out_ref, weight_ref = refs[:RING], refs[RING], refs[RING + 1]
    y, z, core = lax.axis_index("y"), lax.axis_index("z"), lax.axis_index("core")
    mine = jnp.where(core == 0, y, z)
    outer = jnp.where(core == 0, RING, 1)
    inner = jnp.where(core == 0, 1, RING)
    for step in range(RING):
        source = lax.rem(mine + RING - step, RING)
        for i in range(RING):
            weight_ref[source * outer + i * inner] = parts[step][i]

    def order(shape, axis):
        i = lax.broadcasted_iota(jnp.int32, shape, axis)
        piece = (i >= COUNT // 2).astype(jnp.int32)
        j = i - piece * (COUNT // 2)
        source = (j * 3277) >> 16
        return source * (2 * CAP) + piece * CAP + j - source * CAP

    square = (COUNT, COUNT)
    take = (lax.broadcasted_iota(jnp.int32, square, 1) == order((COUNT, 1), 0)).astype(jnp.bfloat16)
    give = (lax.broadcasted_iota(jnp.int32, square, 0) == order((1, COUNT), 1)).astype(jnp.bfloat16)
    rows = jnp.dot(take, got_ref[...], preferred_element_type=jnp.float32).astype(jnp.bfloat16)
    half = RING * RING // 2
    width = weight_ref.shape[1] * half
    back = jnp.dot(
        rows[: COUNT // 2], weight_ref[:half].reshape(width, FFW), preferred_element_type=jnp.float32
    ) + jnp.dot(
        rows[COUNT // 2 :], weight_ref[half:].reshape(width, FFW), preferred_element_type=jnp.float32
    )
    back = back.astype(jnp.bfloat16)
    back = jnp.concatenate([back[:, : FFW // 2], back[:, FFW // 2 :]], axis=0)
    out_ref[...] = jnp.dot(give, back, preferred_element_type=jnp.float32).astype(jnp.bfloat16)


def onehot(index, rows):
    return (jnp.arange(rows, dtype=jnp.int32)[:, None] == index[None, :]).astype(jnp.bfloat16)


def body(cotangent, gate_up, route_probs, routes, down_weight):
    tokens = cotangent.shape[0]

    own = down_weight[0]
    line = lax.all_to_all(
        jnp.broadcast_to(own[None], (RING,) + own.shape),
        TORUS,
        split_axis=0,
        concat_axis=0,
        axis_index_groups=first_groups(),
        tiled=True,
    )
    parts = [line] + [lax.ppermute(line, TORUS, second_shift(step)) for step in range(1, RING)]

    flat_routes = routes.reshape(tokens)
    member = (flat_routes[:, None] == jnp.arange(EXPERTS, dtype=jnp.int32)[None, :]).astype(jnp.int32)
    rank = jnp.sum(jnp.cumsum(member, axis=0) * member, axis=1) - 1
    first = flat_routes * (2 * CAP) + rank
    both = jnp.concatenate([first, first + CAP])
    placing = onehot(both, EXPERTS * 2 * CAP)
    quarters = [cotangent[:, i * QUART : (i + 1) * QUART] for i in range(4)]
    sent = jnp.stack(
        [
            jnp.dot(
                placing,
                jnp.concatenate([quarters[2 * h], quarters[2 * h + 1]], axis=0),
                preferred_element_type=jnp.float32,
            ).astype(jnp.bfloat16)
            for h in range(2)
        ]
    ).reshape(PEERS, 2 * CAP, QUART)
    got = lax.all_to_all(sent, SHARE, split_axis=0, concat_axis=0, tiled=True)

    back = pl.pallas_call(
        product,
        out_shape=jax.ShapeDtypeStruct((COUNT, FFW // 2), jnp.bfloat16),
        in_specs=[pl.BlockSpec(memory_space=pltpu.VMEM)] * (RING + 1),
        out_specs=pl.BlockSpec(memory_space=pltpu.VMEM),
        scratch_shapes=[pltpu.VMEM((RING * RING,) + own.shape, jnp.bfloat16)],
        compiler_params=pltpu.CompilerParams(vmem_limit_bytes=20 * 2**20),
        cost_estimate=pl.CostEstimate(flops=2 * 10**9, bytes_accessed=10**7, transcendentals=0),
    )(got.reshape(COUNT, QUART), *parts)
    came = lax.all_to_all(
        back.reshape(PEERS, 2 * CAP, FFW // 2), SHARE, split_axis=0, concat_axis=0, tiled=True
    ).reshape(COUNT, FFW // 2)

    place = jnp.arange(COUNT, dtype=jnp.int32) % (COUNT // 2)
    back_hidden = jnp.concatenate(
        [
            jnp.dot(
                (place[None, :] == (first + c * CAP)[:, None]).astype(jnp.bfloat16),
                came,
                preferred_element_type=jnp.float32,
            )
            for c in range(2)
        ],
        axis=1,
    )

    flat_pre = gate_up.reshape(tokens, 2 * FFW)
    gate = flat_pre[:, :FFW].astype(jnp.float32)
    up = flat_pre[:, FFW:].astype(jnp.float32)
    squash = jax.nn.sigmoid(gate)
    hidden = (gate * squash * up).astype(jnp.bfloat16).astype(jnp.float32)
    grad_probs = jnp.sum(hidden * back_hidden, axis=1, keepdims=True).astype(jnp.bfloat16)
    scaled = route_probs.astype(jnp.float32) * back_hidden
    grad_gate = scaled * up * squash * (1.0 + gate * (1.0 - squash))
    grad_up = scaled * gate * squash
    grads = jnp.concatenate([grad_gate, grad_up], axis=-1).astype(jnp.bfloat16)
    return grads.reshape(tokens, 1, 2 * FFW), grad_probs


def solution(mesh):
    named = Mesh(mesh.devices.reshape(2, 8, 8, 4, 2), AXES)
    return jax.shard_map(
        body,
        mesh=named,
        in_specs=(
            P(AXES, None),
            P(AXES, None, None),
            P(AXES, None),
            P(AXES, None),
            P(("xh", "core"), ("xl", "y", "z"), None),
        ),
        out_specs=(P(AXES, None, None), P(AXES, None)),
        check_vma=False,
    )
```

```python
import jax
import jax.numpy as jnp
from jax import lax
from jax.experimental import pallas as pl
from jax.experimental.pallas import tpu as pltpu
from jax.sharding import Mesh, PartitionSpec as P

D = 4096
FFW = 768
HALF = D // 2
QUART = D // 4
EXPERTS = 8
CAP = 20
PEERS = 16

AXES = ("xl", "y", "z", "xh", "core")
SHARE = ("xl", "xh", "core")

TORUS = ("y", "z", "xh", "core")
RING = 8
LINES = [(h, c) for h in range(4) for c in range(2)]
COUNT = PEERS * 2 * CAP


def place_of(y, z, h, c):
    return (((y % RING) * RING + z % RING) * 4 + h) * 2 + c


def first_groups():
    return [
        [place_of(k, i, h, c) if c == 0 else place_of(i, k, h, c) for i in range(RING)]
        for h, c in LINES
        for k in range(RING)
    ]


def second_shift(step):
    return [
        (place_of(y, z, h, c), place_of(y + step, z, h, c) if c == 0 else place_of(y, z + step, h, c))
        for y in range(RING)
        for z in range(RING)
        for h, c in LINES
    ]


HALF_RING = RING // 2
PIECES = (
    (0, 0, RING, 0, 0),
    (1, 0, RING, 3, 0),
    (2, 0, RING, -3, 0),
    (3, 0, RING, -1, 0),
    (3, RING, RING, 2, 0),
    (3, 2 * RING, HALF_RING, 4, 0),
    (4, 0, RING, 1, 0),
    (4, RING, RING, -2, 0),
    (4, 2 * RING, HALF_RING, 4, HALF_RING),
)
ARRAYS = 5


def product(got_ref, *refs):
    parts, out_ref, weight_ref, sems = refs[:ARRAYS], refs[ARRAYS], refs[ARRAYS + 1], refs[ARRAYS + 2]
    y, z, core = lax.axis_index("y"), lax.axis_index("z"), lax.axis_index("core")

    def copies(along_y):
        out = []
        for n, (which, first, blocks, offset, at) in enumerate(PIECES):
            source = lax.rem((y if along_y else z) + offset + RING, RING)
            dst = weight_ref.at[source, at : at + blocks] if along_y else weight_ref.at[at : at + blocks, source]
            out.append(pltpu.make_async_copy(parts[which].at[first : first + blocks], dst, sems.at[n]))
        return out

    @pl.when(core == 0)
    def _():
        for copy in copies(True):
            copy.start()

    @pl.when(core != 0)
    def _():
        for copy in copies(False):
            copy.start()

    def order(shape, axis):
        i = lax.broadcasted_iota(jnp.int32, shape, axis)
        piece = (i >= COUNT // 2).astype(jnp.int32)
        j = i - piece * (COUNT // 2)
        source = (j * 3277) >> 16
        return source * (2 * CAP) + piece * CAP + j - source * CAP

    square = (COUNT, COUNT)
    take = (lax.broadcasted_iota(jnp.int32, square, 1) == order((COUNT, 1), 0)).astype(jnp.bfloat16)
    give = (lax.broadcasted_iota(jnp.int32, square, 0) == order((1, COUNT), 1)).astype(jnp.bfloat16)
    rows = jnp.dot(take, got_ref[...], preferred_element_type=jnp.float32).astype(jnp.bfloat16)

    @pl.when(core == 0)
    def _():
        for copy in copies(True):
            copy.wait()

    @pl.when(core != 0)
    def _():
        for copy in copies(False):
            copy.wait()

    half = RING // 2
    width = weight_ref.shape[2] * RING * half
    back = jnp.dot(
        rows[: COUNT // 2], weight_ref[:half].reshape(width, FFW), preferred_element_type=jnp.float32
    ) + jnp.dot(
        rows[COUNT // 2 :], weight_ref[half:].reshape(width, FFW), preferred_element_type=jnp.float32
    )
    back = back.astype(jnp.bfloat16)
    back = jnp.concatenate([back[:, : FFW // 2], back[:, FFW // 2 :]], axis=0)
    out_ref[...] = jnp.dot(give, back, preferred_element_type=jnp.float32).astype(jnp.bfloat16)


def onehot(index, rows):
    return (jnp.arange(rows, dtype=jnp.int32)[:, None] == index[None, :]).astype(jnp.bfloat16)


def body(cotangent, gate_up, route_probs, routes, down_weight):
    tokens = cotangent.shape[0]

    own = down_weight[0]
    line = lax.all_to_all(
        jnp.broadcast_to(own[None], (RING,) + own.shape),
        TORUS,
        split_axis=0,
        concat_axis=0,
        axis_index_groups=first_groups(),
        tiled=True,
    )
    ahead = lax.ppermute(line, TORUS, second_shift(-3))
    behind = lax.ppermute(line, TORUS, second_shift(3))
    up = jnp.concatenate([line, ahead, behind[:HALF_RING]], axis=0)
    down = jnp.concatenate([line, behind, ahead[HALF_RING:]], axis=0)
    parts = [line, ahead, behind, lax.ppermute(up, TORUS, second_shift(1)), lax.ppermute(down, TORUS, second_shift(-1))]

    flat_routes = routes.reshape(tokens)
    member = (flat_routes[:, None] == jnp.arange(EXPERTS, dtype=jnp.int32)[None, :]).astype(jnp.int32)
    rank = jnp.sum(jnp.cumsum(member, axis=0) * member, axis=1) - 1
    first = flat_routes * (2 * CAP) + rank
    both = jnp.concatenate([first, first + CAP])
    placing = onehot(both, EXPERTS * 2 * CAP)
    quarters = [cotangent[:, i * QUART : (i + 1) * QUART] for i in range(4)]
    sent = jnp.stack(
        [
            jnp.dot(
                placing,
                jnp.concatenate([quarters[2 * h], quarters[2 * h + 1]], axis=0),
                preferred_element_type=jnp.float32,
            ).astype(jnp.bfloat16)
            for h in range(2)
        ]
    ).reshape(PEERS, 2 * CAP, QUART)
    got = lax.all_to_all(sent, SHARE, split_axis=0, concat_axis=0, tiled=True)

    back = pl.pallas_call(
        product,
        out_shape=jax.ShapeDtypeStruct((COUNT, FFW // 2), jnp.bfloat16),
        in_specs=[pl.BlockSpec(memory_space=pltpu.VMEM)] + [pl.BlockSpec(memory_space=pl.ANY)] * ARRAYS,
        out_specs=pl.BlockSpec(memory_space=pltpu.VMEM),
        scratch_shapes=[
            pltpu.VMEM((RING, RING) + own.shape, jnp.bfloat16),
            pltpu.SemaphoreType.DMA((len(PIECES),)),
        ],
        compiler_params=pltpu.CompilerParams(vmem_limit_bytes=20 * 2**20),
        cost_estimate=pl.CostEstimate(flops=2 * 10**9, bytes_accessed=10**7, transcendentals=0),
    )(got.reshape(COUNT, QUART), *parts)
    came = lax.all_to_all(
        back.reshape(PEERS, 2 * CAP, FFW // 2), SHARE, split_axis=0, concat_axis=0, tiled=True
    ).reshape(COUNT, FFW // 2)

    place = jnp.arange(COUNT, dtype=jnp.int32) % (COUNT // 2)
    back_hidden = jnp.concatenate(
        [
            jnp.dot(
                (place[None, :] == (first + c * CAP)[:, None]).astype(jnp.bfloat16),
                came,
                preferred_element_type=jnp.float32,
            )
            for c in range(2)
        ],
        axis=1,
    )

    flat_pre = gate_up.reshape(tokens, 2 * FFW)
    gate = flat_pre[:, :FFW].astype(jnp.float32)
    up = flat_pre[:, FFW:].astype(jnp.float32)
    squash = jax.nn.sigmoid(gate)
    hidden = (gate * squash * up).astype(jnp.bfloat16).astype(jnp.float32)
    grad_probs = jnp.sum(hidden * back_hidden, axis=1, keepdims=True).astype(jnp.bfloat16)
    scaled = route_probs.astype(jnp.float32) * back_hidden
    grad_gate = scaled * up * squash * (1.0 + gate * (1.0 - squash))
    grad_up = scaled * gate * squash
    grads = jnp.concatenate([grad_gate, grad_up], axis=-1).astype(jnp.bfloat16)
    return grads.reshape(tokens, 1, 2 * FFW), grad_probs


def solution(mesh):
    named = Mesh(mesh.devices.reshape(2, 8, 8, 4, 2), AXES)
    return jax.shard_map(
        body,
        mesh=named,
        in_specs=(
            P(AXES, None),
            P(AXES, None, None),
            P(AXES, None),
            P(AXES, None),
            P(("xh", "core"), ("xl", "y", "z"), None),
        ),
        out_specs=(P(AXES, None, None), P(AXES, None)),
        check_vma=False,
    )
```

```python
import jax
import jax.numpy as jnp
from jax import lax
from jax.experimental import pallas as pl
from jax.experimental.pallas import tpu as pltpu
from jax.sharding import Mesh, PartitionSpec as P

D = 4096
FFW = 768
HALF = D // 2
QUART = D // 4
EXPERTS = 8
CAP = 20
PEERS = 16

AXES = ("xl", "y", "z", "xh", "core")
SHARE = ("xl", "xh", "core")

TORUS = ("y", "z", "xh", "core")
RING = 8
HALF_RING = RING // 2
LINES = [(h, c) for h in range(4) for c in range(2)]
COUNT = PEERS * 2 * CAP


def place_of(y, z, h, c):
    return (((y % RING) * RING + z % RING) * 4 + h) * 2 + c


def first_groups():
    return [
        [
            place_of(k + far, i, h, c) if c == 0 else place_of(i, k + far, h, c)
            for far in (0, HALF_RING)
            for i in range(RING)
        ]
        for h, c in LINES
        for k in range(HALF_RING)
    ]


def second_shift(step):
    return [
        (place_of(y, z, h, c), place_of(y + step, z, h, c) if c == 0 else place_of(y, z + step, h, c))
        for y in range(RING)
        for z in range(RING)
        for h, c in LINES
    ]


PIECES = (
    (0, 0, 0, 0),
    (0, RING, 0, 1),
    (1, 0, 1, 0),
    (1, RING, 1, 1),
    (2, 0, -1, 0),
    (2, RING, -1, 1),
    (3, 0, 2, 0),
    (4, 0, 2, 1),
)
ARRAYS = 5


def product(rows_ref, *refs):
    parts, out_ref, weight_ref = refs[:ARRAYS], refs[ARRAYS], refs[ARRAYS + 1]
    y, z, core = lax.axis_index("y"), lax.axis_index("z"), lax.axis_index("core")
    mine = jnp.where(core == 0, y, z)
    outer = jnp.where(core == 0, RING, 1)
    inner = jnp.where(core == 0, 1, RING)
    for which, first, offset, far in PIECES:
        source = lax.rem(mine + offset + RING, HALF_RING) + far * HALF_RING
        for i in range(RING):
            weight_ref[source * outer + i * inner] = parts[which][first + i]

    half = RING * RING // 2
    width = weight_ref.shape[1] * half
    back = jnp.dot(
        rows_ref[: COUNT // 2], weight_ref[:half].reshape(width, FFW), preferred_element_type=jnp.float32
    ) + jnp.dot(
        rows_ref[COUNT // 2 :], weight_ref[half:].reshape(width, FFW), preferred_element_type=jnp.float32
    )
    back = back.astype(jnp.bfloat16)
    back = jnp.concatenate([back[:, : FFW // 2], back[:, FFW // 2 :]], axis=0)

    i = lax.broadcasted_iota(jnp.int32, (1, COUNT), 1)
    piece = (i >= COUNT // 2).astype(jnp.int32)
    j = i - piece * (COUNT // 2)
    source = (j * 3277) >> 16
    order = source * (2 * CAP) + piece * CAP + j - source * CAP
    give = (lax.broadcasted_iota(jnp.int32, (COUNT, COUNT), 0) == order).astype(jnp.bfloat16)
    out_ref[...] = jnp.dot(give, back, preferred_element_type=jnp.float32).astype(jnp.bfloat16)


def onehot(index, rows):
    return (jnp.arange(rows, dtype=jnp.int32)[:, None] == index[None, :]).astype(jnp.bfloat16)


def body(cotangent, gate_up, route_probs, routes, down_weight):
    tokens = cotangent.shape[0]

    own = down_weight[0]
    lines = lax.all_to_all(
        jnp.broadcast_to(own[None], (2 * RING,) + own.shape),
        TORUS,
        split_axis=0,
        concat_axis=0,
        axis_index_groups=first_groups(),
        tiled=True,
    )
    parts = [
        lines,
        lax.ppermute(lines, TORUS, second_shift(-1)),
        lax.ppermute(lines, TORUS, second_shift(1)),
        lax.ppermute(lines[:RING], TORUS, second_shift(-2)),
        lax.ppermute(lines[RING:], TORUS, second_shift(2)),
    ]

    flat_routes = routes.reshape(tokens)
    member = (flat_routes[:, None] == jnp.arange(EXPERTS, dtype=jnp.int32)[None, :]).astype(jnp.int32)
    rank = jnp.sum(jnp.cumsum(member, axis=0) * member, axis=1) - 1
    first = flat_routes * (2 * CAP) + rank
    both = jnp.concatenate([first, first + CAP])
    placing = onehot(both, EXPERTS * 2 * CAP)
    quarters = [cotangent[:, i * QUART : (i + 1) * QUART] for i in range(4)]
    sent = jnp.stack(
        [
            jnp.dot(
                placing,
                jnp.concatenate([quarters[2 * h], quarters[2 * h + 1]], axis=0),
                preferred_element_type=jnp.float32,
            ).astype(jnp.bfloat16)
            for h in range(2)
        ]
    ).reshape(PEERS, 2 * CAP, QUART)
    got = lax.all_to_all(sent, SHARE, split_axis=0, concat_axis=0, tiled=True)

    order = jnp.arange(COUNT, dtype=jnp.int32)
    order = (order % (COUNT // 2)) // CAP * (2 * CAP) + order // (COUNT // 2) * CAP + order % CAP
    take = (order[:, None] == jnp.arange(COUNT, dtype=jnp.int32)[None, :]).astype(jnp.bfloat16)
    rows = jnp.dot(take, got.reshape(COUNT, QUART), preferred_element_type=jnp.float32).astype(jnp.bfloat16)
    back = pl.pallas_call(
        product,
        out_shape=jax.ShapeDtypeStruct((COUNT, FFW // 2), jnp.bfloat16),
        in_specs=[pl.BlockSpec(memory_space=pltpu.VMEM)] * (ARRAYS + 1),
        out_specs=pl.BlockSpec(memory_space=pltpu.VMEM),
        scratch_shapes=[pltpu.VMEM((RING * RING,) + own.shape, jnp.bfloat16)],
        compiler_params=pltpu.CompilerParams(vmem_limit_bytes=20 * 2**20),
        cost_estimate=pl.CostEstimate(flops=2 * 10**9, bytes_accessed=10**7, transcendentals=0),
    )(rows, *parts)
    came = lax.all_to_all(
        back.reshape(PEERS, 2 * CAP, FFW // 2), SHARE, split_axis=0, concat_axis=0, tiled=True
    ).reshape(COUNT, FFW // 2)

    place = jnp.arange(COUNT, dtype=jnp.int32) % (COUNT // 2)
    back_hidden = jnp.concatenate(
        [
            jnp.dot(
                (place[None, :] == (first + c * CAP)[:, None]).astype(jnp.bfloat16),
                came,
                preferred_element_type=jnp.float32,
            )
            for c in range(2)
        ],
        axis=1,
    )

    flat_pre = gate_up.reshape(tokens, 2 * FFW)
    gate = flat_pre[:, :FFW].astype(jnp.float32)
    up = flat_pre[:, FFW:].astype(jnp.float32)
    squash = jax.nn.sigmoid(gate)
    hidden = (gate * squash * up).astype(jnp.bfloat16).astype(jnp.float32)
    grad_probs = jnp.sum(hidden * back_hidden, axis=1, keepdims=True).astype(jnp.bfloat16)
    scaled = route_probs.astype(jnp.float32) * back_hidden
    grad_gate = scaled * up * squash * (1.0 + gate * (1.0 - squash))
    grad_up = scaled * gate * squash
    grads = jnp.concatenate([grad_gate, grad_up], axis=-1).astype(jnp.bfloat16)
    return grads.reshape(tokens, 1, 2 * FFW), grad_probs


def solution(mesh):
    named = Mesh(mesh.devices.reshape(2, 8, 8, 4, 2), AXES)
    return jax.shard_map(
        body,
        mesh=named,
        in_specs=(
            P(AXES, None),
            P(AXES, None, None),
            P(AXES, None),
            P(AXES, None),
            P(("xh", "core"), ("xl", "y", "z"), None),
        ),
        out_specs=(P(AXES, None, None), P(AXES, None)),
        check_vma=False,
    )
```

```python
import jax
import jax.numpy as jnp
from jax import lax
from jax.experimental import pallas as pl
from jax.experimental.pallas import tpu as pltpu
from jax.sharding import Mesh, PartitionSpec as P

D = 4096
FFW = 768
HALF = D // 2
QUART = D // 4
EXPERTS = 8
CAP = 20
PEERS = 16

AXES = ("xl", "y", "z", "xh", "core")
SHARE = ("xl", "xh", "core")

TORUS = ("y", "z", "xh", "core")
RING = 8
HALF_RING = RING // 2
LINES = [(h, c) for h in range(4) for c in range(2)]
COUNT = PEERS * 2 * CAP


def place_of(y, z, h, c):
    return (((y % RING) * RING + z % RING) * 4 + h) * 2 + c


def first_groups():
    return [
        [place_of(k, i, h, c) if c == 0 else place_of(i, k, h, c) for i in range(RING)]
        for h, c in LINES
        for k in range(RING)
    ]


def second_shift(step):
    return [
        (place_of(y, z, h, c), place_of(y + step, z, h, c) if c == 0 else place_of(y, z + step, h, c))
        for y in range(RING)
        for z in range(RING)
        for h, c in LINES
    ]


PIECES = (
    (0, 0, RING, 0, 0),
    (1, 0, RING, 3, 0),
    (2, 0, RING, -3, 0),
    (3, 0, RING, -1, 0),
    (3, RING, RING, 2, 0),
    (3, 2 * RING, HALF_RING, 4, 0),
    (4, 0, RING, 1, 0),
    (4, RING, RING, -2, 0),
    (4, 2 * RING, HALF_RING, 4, HALF_RING),
)
ARRAYS = 5


def product(rows_ref, *refs):
    parts, out_ref, weight_ref = refs[:ARRAYS], refs[ARRAYS], refs[ARRAYS + 1]
    y, z, core = lax.axis_index("y"), lax.axis_index("z"), lax.axis_index("core")
    mine = jnp.where(core == 0, y, z)
    outer = jnp.where(core == 0, RING, 1)
    inner = jnp.where(core == 0, 1, RING)
    for which, first, blocks, offset, at in PIECES:
        source = lax.rem(mine + offset + RING, RING)
        for i in range(blocks):
            weight_ref[source * outer + (at + i) * inner] = parts[which][first + i]

    half = RING * RING // 2
    width = weight_ref.shape[1] * half
    back = jnp.dot(
        rows_ref[: COUNT // 2], weight_ref[:half].reshape(width, FFW), preferred_element_type=jnp.float32
    ) + jnp.dot(
        rows_ref[COUNT // 2 :], weight_ref[half:].reshape(width, FFW), preferred_element_type=jnp.float32
    )
    back = back.astype(jnp.bfloat16)
    back = jnp.concatenate([back[:, : FFW // 2], back[:, FFW // 2 :]], axis=0)

    i = lax.broadcasted_iota(jnp.int32, (1, COUNT), 1)
    piece = (i >= COUNT // 2).astype(jnp.int32)
    j = i - piece * (COUNT // 2)
    source = (j * 3277) >> 16
    order = source * (2 * CAP) + piece * CAP + j - source * CAP
    give = (lax.broadcasted_iota(jnp.int32, (COUNT, COUNT), 0) == order).astype(jnp.bfloat16)
    out_ref[...] = jnp.dot(give, back, preferred_element_type=jnp.float32).astype(jnp.bfloat16)


def onehot(index, rows):
    return (jnp.arange(rows, dtype=jnp.int32)[:, None] == index[None, :]).astype(jnp.bfloat16)


def body(cotangent, gate_up, route_probs, routes, down_weight):
    tokens = cotangent.shape[0]

    own = down_weight[0]
    line = lax.all_to_all(
        jnp.broadcast_to(own[None], (RING,) + own.shape),
        TORUS,
        split_axis=0,
        concat_axis=0,
        axis_index_groups=first_groups(),
        tiled=True,
    )
    ahead = lax.ppermute(line, TORUS, second_shift(-3))
    behind = lax.ppermute(line, TORUS, second_shift(3))
    up = jnp.concatenate([line, ahead, behind[:HALF_RING]], axis=0)
    down = jnp.concatenate([line, behind, ahead[HALF_RING:]], axis=0)
    parts = [line, ahead, behind, lax.ppermute(up, TORUS, second_shift(1)), lax.ppermute(down, TORUS, second_shift(-1))]

    flat_routes = routes.reshape(tokens)
    member = (flat_routes[:, None] == jnp.arange(EXPERTS, dtype=jnp.int32)[None, :]).astype(jnp.int32)
    rank = jnp.sum(jnp.cumsum(member, axis=0) * member, axis=1) - 1
    first = flat_routes * (2 * CAP) + rank
    both = jnp.concatenate([first, first + CAP])
    placing = onehot(both, EXPERTS * 2 * CAP)
    quarters = [cotangent[:, i * QUART : (i + 1) * QUART] for i in range(4)]
    sent = jnp.stack(
        [
            jnp.dot(
                placing,
                jnp.concatenate([quarters[2 * h], quarters[2 * h + 1]], axis=0),
                preferred_element_type=jnp.float32,
            ).astype(jnp.bfloat16)
            for h in range(2)
        ]
    ).reshape(PEERS, 2 * CAP, QUART)
    got = lax.all_to_all(sent, SHARE, split_axis=0, concat_axis=0, tiled=True)

    order = jnp.arange(COUNT, dtype=jnp.int32)
    order = (order % (COUNT // 2)) // CAP * (2 * CAP) + order // (COUNT // 2) * CAP + order % CAP
    take = (order[:, None] == jnp.arange(COUNT, dtype=jnp.int32)[None, :]).astype(jnp.bfloat16)
    rows = jnp.dot(take, got.reshape(COUNT, QUART), preferred_element_type=jnp.float32).astype(jnp.bfloat16)
    back = pl.pallas_call(
        product,
        out_shape=jax.ShapeDtypeStruct((COUNT, FFW // 2), jnp.bfloat16),
        in_specs=[pl.BlockSpec(memory_space=pltpu.VMEM)] * (ARRAYS + 1),
        out_specs=pl.BlockSpec(memory_space=pltpu.VMEM),
        scratch_shapes=[pltpu.VMEM((RING * RING,) + own.shape, jnp.bfloat16)],
        compiler_params=pltpu.CompilerParams(vmem_limit_bytes=20 * 2**20),
        cost_estimate=pl.CostEstimate(flops=2 * 10**9, bytes_accessed=10**7, transcendentals=0),
    )(rows, *parts)
    came = lax.all_to_all(
        back.reshape(PEERS, 2 * CAP, FFW // 2), SHARE, split_axis=0, concat_axis=0, tiled=True
    ).reshape(COUNT, FFW // 2)

    place = jnp.arange(COUNT, dtype=jnp.int32) % (COUNT // 2)
    back_hidden = jnp.concatenate(
        [
            jnp.dot(
                (place[None, :] == (first + c * CAP)[:, None]).astype(jnp.bfloat16),
                came,
                preferred_element_type=jnp.float32,
            )
            for c in range(2)
        ],
        axis=1,
    )

    flat_pre = gate_up.reshape(tokens, 2 * FFW)
    gate = flat_pre[:, :FFW].astype(jnp.float32)
    up = flat_pre[:, FFW:].astype(jnp.float32)
    squash = jax.nn.sigmoid(gate)
    hidden = (gate * squash * up).astype(jnp.bfloat16).astype(jnp.float32)
    grad_probs = jnp.sum(hidden * back_hidden, axis=1, keepdims=True).astype(jnp.bfloat16)
    scaled = route_probs.astype(jnp.float32) * back_hidden
    grad_gate = scaled * up * squash * (1.0 + gate * (1.0 - squash))
    grad_up = scaled * gate * squash
    grads = jnp.concatenate([grad_gate, grad_up], axis=-1).astype(jnp.bfloat16)
    return grads.reshape(tokens, 1, 2 * FFW), grad_probs


def solution(mesh):
    named = Mesh(mesh.devices.reshape(2, 8, 8, 4, 2), AXES)
    return jax.shard_map(
        body,
        mesh=named,
        in_specs=(
            P(AXES, None),
            P(AXES, None, None),
            P(AXES, None),
            P(AXES, None),
            P(("xh", "core"), ("xl", "y", "z"), None),
        ),
        out_specs=(P(AXES, None, None), P(AXES, None)),
        check_vma=False,
    )
```

```python
import jax
import jax.numpy as jnp
from jax import lax
from jax.experimental import pallas as pl
from jax.experimental.pallas import tpu as pltpu
from jax.sharding import Mesh, PartitionSpec as P

D = 4096
FFW = 768
HALF = D // 2
EXPERTS = 8
CAP = 20
PEERS = 16

AXES = ("xl", "y", "z", "xh", "core")
SHARE = ("xl", "xh", "core")

TORUS = ("y", "z", "xh", "core")
RING = 8
HALF_RING = RING // 2
LINES = [(h, c) for h in range(4) for c in range(2)]
COUNT = PEERS * 2 * CAP


def place_of(y, z, h, c):
    return (((y % RING) * RING + z % RING) * 4 + h) * 2 + c


def first_groups():
    return [
        [place_of(k, i, h, c) if c == 0 else place_of(i, k, h, c) for i in range(RING)]
        for h, c in LINES
        for k in range(RING)
    ]


def second_shift(step):
    return [
        (place_of(y, z, h, c), place_of(y + step, z, h, c) if c == 0 else place_of(y, z + step, h, c))
        for y in range(RING)
        for z in range(RING)
        for h, c in LINES
    ]


PIECES = (
    (0, 0, RING, 0, 0),
    (1, 0, RING, 3, 0),
    (2, 0, RING, -3, 0),
    (3, 0, RING, -1, 0),
    (3, RING, RING, 2, 0),
    (3, 2 * RING, HALF_RING, 4, 0),
    (4, 0, RING, 1, 0),
    (4, RING, RING, -2, 0),
    (4, 2 * RING, HALF_RING, 4, HALF_RING),
)
ARRAYS = 5


def product(rows_ref, *refs):
    parts, out_ref, weight_ref = refs[:ARRAYS], refs[ARRAYS], refs[ARRAYS + 1]
    y, z, core = lax.axis_index("y"), lax.axis_index("z"), lax.axis_index("core")
    mine = jnp.where(core == 0, y, z)
    outer = jnp.where(core == 0, RING, 1)
    inner = jnp.where(core == 0, 1, RING)
    for which, first, blocks, offset, at in PIECES:
        source = lax.rem(mine + offset + RING, RING)
        for i in range(blocks):
            weight_ref[source * outer + (at + i) * inner] = parts[which][first + i]

    half = RING * RING // 2
    width = weight_ref.shape[1] * half
    back = jnp.dot(
        rows_ref[:, :width], weight_ref[:half].reshape(width, FFW), preferred_element_type=jnp.float32
    ) + jnp.dot(
        rows_ref[:, width:], weight_ref[half:].reshape(width, FFW), preferred_element_type=jnp.float32
    )
    back = back.astype(jnp.bfloat16)
    back = jnp.concatenate([back[:, : FFW // 2], back[:, FFW // 2 :]], axis=0)

    i = lax.broadcasted_iota(jnp.int32, (1, COUNT), 1)
    columns = (i >= COUNT // 2).astype(jnp.int32)
    j = i - columns * (COUNT // 2)
    source = (j * 1639) >> 16
    j = j - source * (2 * CAP)
    other = (j >= CAP).astype(jnp.int32)
    xl = jnp.where(lax.axis_index("xl") == 0, other, 1 - other)
    order = xl * (COUNT // 2) + source * (2 * CAP) + columns * CAP + j - other * CAP
    give = (lax.broadcasted_iota(jnp.int32, (COUNT, COUNT), 0) == order).astype(jnp.bfloat16)
    out_ref[...] = jnp.dot(give, back, preferred_element_type=jnp.float32).astype(jnp.bfloat16)


def gather_rows(cotangent_ref, came_ref, routes_ref, sent_ref):
    tokens = cotangent_ref.shape[0]
    half = pl.multiple_of(lax.axis_index("xl") * HALF, HALF)
    square = (tokens, tokens)
    before = (
        lax.broadcasted_iota(jnp.int32, square, 0) < lax.broadcasted_iota(jnp.int32, square, 1)
    ).astype(jnp.bfloat16)
    expert = lax.broadcasted_iota(jnp.int32, (2 * EXPERTS, tokens), 0)
    row = lax.broadcasted_iota(jnp.int32, (PEERS * CAP, tokens), 0)

    def placing(routes, other):
        member = expert == routes
        earlier = jnp.dot(member.astype(jnp.bfloat16), before, preferred_element_type=jnp.float32)
        rank = jnp.sum(jnp.where(member, earlier, 0.0), axis=0, keepdims=True).astype(jnp.int32)
        return (row == routes * (2 * CAP) + other * CAP + rank).astype(jnp.bfloat16)

    theirs = came_ref[tokens : tokens + 16, :tokens][:1].astype(jnp.float32).astype(jnp.int32)
    sent_ref[...] = (
        jnp.dot(
            placing(routes_ref[...], 0), cotangent_ref[:, pl.ds(half, HALF)], preferred_element_type=jnp.float32
        )
        + jnp.dot(placing(theirs, 1), came_ref[:tokens], preferred_element_type=jnp.float32)
    ).astype(jnp.bfloat16)


def body(cotangent, gate_up, route_probs, routes, down_weight):
    tokens = cotangent.shape[0]

    own = down_weight[0]
    line = lax.all_to_all(
        jnp.broadcast_to(own[None], (RING,) + own.shape),
        TORUS,
        split_axis=0,
        concat_axis=0,
        axis_index_groups=first_groups(),
        tiled=True,
    )
    ahead = lax.ppermute(line, TORUS, second_shift(-3))
    behind = lax.ppermute(line, TORUS, second_shift(3))
    up = jnp.concatenate([line, ahead, behind[:HALF_RING]], axis=0)
    down = jnp.concatenate([line, behind, ahead[HALF_RING:]], axis=0)
    parts = [line, ahead, behind, lax.ppermute(up, TORUS, second_shift(1)), lax.ppermute(down, TORUS, second_shift(-1))]

    flat_routes = routes.reshape(tokens)
    member = (flat_routes[:, None] == jnp.arange(EXPERTS, dtype=jnp.int32)[None, :]).astype(jnp.int32)
    rank = jnp.sum(jnp.cumsum(member, axis=0) * member, axis=1) - 1
    first = flat_routes * (2 * CAP) + rank

    theirs = lax.dynamic_slice_in_dim(cotangent, (1 - lax.axis_index("xl")) * HALF, HALF, axis=1)
    told = jnp.pad(routes.reshape(1, tokens).astype(jnp.bfloat16), ((0, 15), (0, HALF - tokens)))
    came = lax.ppermute(jnp.concatenate([theirs, told], axis=0), "xl", [(0, 1), (1, 0)])
    sent = pl.pallas_call(
        gather_rows,
        out_shape=jax.ShapeDtypeStruct((PEERS * CAP, HALF), jnp.bfloat16),
        in_specs=[pl.BlockSpec(memory_space=pltpu.VMEM)] * 3,
        out_specs=pl.BlockSpec(memory_space=pltpu.VMEM),
        compiler_params=pltpu.CompilerParams(vmem_limit_bytes=20 * 2**20),
        cost_estimate=pl.CostEstimate(flops=4 * 10**8, bytes_accessed=3 * 10**6, transcendentals=0),
    )(cotangent, came, routes.reshape(1, tokens))
    got = lax.all_to_all(
        sent.reshape(EXPERTS, 2 * CAP, HALF), ("xh", "core"), split_axis=0, concat_axis=0, tiled=True
    )

    rows = jnp.where(lax.axis_index("xl") < 2, got.reshape(PEERS * CAP, HALF), 0)
    back = pl.pallas_call(
        product,
        out_shape=jax.ShapeDtypeStruct((COUNT, FFW // 2), jnp.bfloat16),
        in_specs=[pl.BlockSpec(memory_space=pltpu.VMEM)] * (ARRAYS + 1),
        out_specs=pl.BlockSpec(memory_space=pltpu.VMEM),
        scratch_shapes=[pltpu.VMEM((RING * RING,) + own.shape, jnp.bfloat16)],
        compiler_params=pltpu.CompilerParams(vmem_limit_bytes=20 * 2**20),
        cost_estimate=pl.CostEstimate(flops=2 * 10**9, bytes_accessed=10**7, transcendentals=0),
    )(rows, *parts)
    came = lax.all_to_all(
        back.reshape(PEERS, 2 * CAP, FFW // 2), SHARE, split_axis=0, concat_axis=0, tiled=True
    ).reshape(COUNT, FFW // 2)

    place = jnp.arange(COUNT, dtype=jnp.int32) % (COUNT // 2)
    back_hidden = jnp.concatenate(
        [
            jnp.dot(
                (place[None, :] == (first + c * CAP)[:, None]).astype(jnp.bfloat16),
                came,
                preferred_element_type=jnp.float32,
            )
            for c in range(2)
        ],
        axis=1,
    )

    flat_pre = gate_up.reshape(tokens, 2 * FFW)
    gate = flat_pre[:, :FFW].astype(jnp.float32)
    up = flat_pre[:, FFW:].astype(jnp.float32)
    squash = jax.nn.sigmoid(gate)
    hidden = (gate * squash * up).astype(jnp.bfloat16).astype(jnp.float32)
    grad_probs = jnp.sum(hidden * back_hidden, axis=1, keepdims=True).astype(jnp.bfloat16)
    scaled = route_probs.astype(jnp.float32) * back_hidden
    grad_gate = scaled * up * squash * (1.0 + gate * (1.0 - squash))
    grad_up = scaled * gate * squash
    grads = jnp.concatenate([grad_gate, grad_up], axis=-1).astype(jnp.bfloat16)
    return grads.reshape(tokens, 1, 2 * FFW), grad_probs


def solution(mesh):
    named = Mesh(mesh.devices.reshape(2, 8, 8, 4, 2), AXES)
    return jax.shard_map(
        body,
        mesh=named,
        in_specs=(
            P(AXES, None),
            P(AXES, None, None),
            P(AXES, None),
            P(AXES, None),
            P(("xh", "core"), ("xl", "y", "z"), None),
        ),
        out_specs=(P(AXES, None, None), P(AXES, None)),
        check_vma=False,
    )
```

```python
import jax
import jax.numpy as jnp
from jax import lax
from jax.experimental import pallas as pl
from jax.experimental.pallas import tpu as pltpu
from jax.sharding import Mesh, PartitionSpec as P

D = 4096
FFW = 768
HALF = D // 2
QUART = D // 4
EXPERTS = 8
CAP = 20
PEERS = 16

AXES = ("xl", "y", "z", "xh", "core")
SHARE = ("xl", "xh", "core")

TORUS = ("y", "z", "xh", "core")
RING = 8
HALF_RING = RING // 2
LINES = [(h, c) for h in range(4) for c in range(2)]
COUNT = PEERS * 2 * CAP


def place_of(y, z, h, c):
    return (((y % RING) * RING + z % RING) * 4 + h) * 2 + c


def first_groups():
    return [
        [place_of(k, i, h, c) if c == 0 else place_of(i, k, h, c) for i in range(RING)]
        for h, c in LINES
        for k in range(RING)
    ]


def second_shift(step):
    return [
        (place_of(y, z, h, c), place_of(y + step, z, h, c) if c == 0 else place_of(y, z + step, h, c))
        for y in range(RING)
        for z in range(RING)
        for h, c in LINES
    ]


PIECES = (
    (0, 0, RING, 0, 0),
    (1, 0, RING, 3, 0),
    (2, 0, RING, -3, 0),
    (3, 0, RING, -1, 0),
    (3, RING, RING, 2, 0),
    (3, 2 * RING, HALF_RING, 4, 0),
    (4, 0, RING, 1, 0),
    (4, RING, RING, -2, 0),
    (4, 2 * RING, HALF_RING, 4, HALF_RING),
)
ARRAYS = 5


def product(rows_ref, *refs):
    parts, out_ref, weight_ref = refs[:ARRAYS], refs[ARRAYS], refs[ARRAYS + 1]
    y, z, core = lax.axis_index("y"), lax.axis_index("z"), lax.axis_index("core")
    mine = jnp.where(core == 0, y, z)
    outer = jnp.where(core == 0, RING, 1)
    inner = jnp.where(core == 0, 1, RING)
    for which, first, blocks, offset, at in PIECES:
        source = lax.rem(mine + offset + RING, RING)
        for i in range(blocks):
            weight_ref[source * outer + (at + i) * inner] = parts[which][first + i]

    half = RING * RING // 2
    width = weight_ref.shape[1] * half
    back = jnp.dot(
        rows_ref[: COUNT // 2], weight_ref[:half].reshape(width, FFW), preferred_element_type=jnp.float32
    ) + jnp.dot(
        rows_ref[COUNT // 2 :], weight_ref[half:].reshape(width, FFW), preferred_element_type=jnp.float32
    )
    back = back.astype(jnp.bfloat16)
    back = jnp.concatenate([back[:, : FFW // 2], back[:, FFW // 2 :]], axis=0)

    i = lax.broadcasted_iota(jnp.int32, (1, COUNT), 1)
    piece = (i >= COUNT // 2).astype(jnp.int32)
    j = i - piece * (COUNT // 2)
    source = (j * 3277) >> 16
    order = source * (2 * CAP) + piece * CAP + j - source * CAP
    give = (lax.broadcasted_iota(jnp.int32, (COUNT, COUNT), 0) == order).astype(jnp.bfloat16)
    out_ref[...] = jnp.dot(give, back, preferred_element_type=jnp.float32).astype(jnp.bfloat16)


def finish(came_ref, pre_ref, probs_ref, first_ref, grads_ref, grad_probs_ref):
    tokens = pre_ref.shape[0]
    square = (tokens, tokens)
    line = lax.broadcasted_iota(jnp.int32, square, 0)
    told = jnp.where(line == 0, first_ref[...].astype(jnp.float32), probs_ref[...].astype(jnp.float32)).T
    first, prob = told[:, :1].astype(jnp.int32), told[:, 1:2]
    place = lax.broadcasted_iota(jnp.int32, (tokens, COUNT), 1)
    place = jnp.where(place >= COUNT // 2, place - COUNT // 2, place)
    total = jnp.zeros((tokens, 1), jnp.float32)
    part = FFW // 2
    for c in range(2):
        back = jnp.dot(
            (place == first + c * CAP).astype(jnp.bfloat16), came_ref[...], preferred_element_type=jnp.float32
        )
        gate = pre_ref[:, c * part : (c + 1) * part].astype(jnp.float32)
        up = pre_ref[:, FFW + c * part : FFW + (c + 1) * part].astype(jnp.float32)
        squash = 1.0 / (1.0 + jnp.exp(-gate))
        silu = gate * squash
        hidden = (silu * up).astype(jnp.bfloat16).astype(jnp.float32)
        total += jnp.sum(hidden * back, axis=1, keepdims=True)
        scaled = prob * back
        grads_ref[:, c * part : (c + 1) * part] = (
            scaled * up * squash * (1.0 + gate * (1.0 - squash))
        ).astype(jnp.bfloat16)
        grads_ref[:, FFW + c * part : FFW + (c + 1) * part] = (scaled * silu).astype(jnp.bfloat16)
    grad_probs_ref[...] = jnp.broadcast_to(total, square).T[:1].astype(jnp.bfloat16)


def onehot(index, rows):
    return (jnp.arange(rows, dtype=jnp.int32)[:, None] == index[None, :]).astype(jnp.bfloat16)


def body(cotangent, gate_up, route_probs, routes, down_weight):
    tokens = cotangent.shape[0]

    own = down_weight[0]
    line = lax.all_to_all(
        jnp.broadcast_to(own[None], (RING,) + own.shape),
        TORUS,
        split_axis=0,
        concat_axis=0,
        axis_index_groups=first_groups(),
        tiled=True,
    )
    ahead = lax.ppermute(line, TORUS, second_shift(-3))
    behind = lax.ppermute(line, TORUS, second_shift(3))
    up = jnp.concatenate([line, ahead, behind[:HALF_RING]], axis=0)
    down = jnp.concatenate([line, behind, ahead[HALF_RING:]], axis=0)
    parts = [line, ahead, behind, lax.ppermute(up, TORUS, second_shift(1)), lax.ppermute(down, TORUS, second_shift(-1))]

    flat_routes = routes.reshape(tokens)
    member = (flat_routes[:, None] == jnp.arange(EXPERTS, dtype=jnp.int32)[None, :]).astype(jnp.int32)
    rank = jnp.sum(jnp.cumsum(member, axis=0) * member, axis=1) - 1
    first = flat_routes * (2 * CAP) + rank
    both = jnp.concatenate([first, first + CAP])
    placing = onehot(both, EXPERTS * 2 * CAP)
    quarters = [cotangent[:, i * QUART : (i + 1) * QUART] for i in range(4)]
    sent = jnp.stack(
        [
            jnp.dot(
                placing,
                jnp.concatenate([quarters[2 * h], quarters[2 * h + 1]], axis=0),
                preferred_element_type=jnp.float32,
            ).astype(jnp.bfloat16)
            for h in range(2)
        ]
    ).reshape(PEERS, 2 * CAP, QUART)
    got = lax.all_to_all(sent, SHARE, split_axis=0, concat_axis=0, tiled=True)

    order = jnp.arange(COUNT, dtype=jnp.int32)
    order = (order % (COUNT // 2)) // CAP * (2 * CAP) + order // (COUNT // 2) * CAP + order % CAP
    take = (order[:, None] == jnp.arange(COUNT, dtype=jnp.int32)[None, :]).astype(jnp.bfloat16)
    rows = jnp.dot(take, got.reshape(COUNT, QUART), preferred_element_type=jnp.float32).astype(jnp.bfloat16)
    back = pl.pallas_call(
        product,
        out_shape=jax.ShapeDtypeStruct((COUNT, FFW // 2), jnp.bfloat16),
        in_specs=[pl.BlockSpec(memory_space=pltpu.VMEM)] * (ARRAYS + 1),
        out_specs=pl.BlockSpec(memory_space=pltpu.VMEM),
        scratch_shapes=[pltpu.VMEM((RING * RING,) + own.shape, jnp.bfloat16)],
        compiler_params=pltpu.CompilerParams(vmem_limit_bytes=20 * 2**20),
        cost_estimate=pl.CostEstimate(flops=2 * 10**9, bytes_accessed=10**7, transcendentals=0),
    )(rows, *parts)
    came = lax.all_to_all(
        back.reshape(PEERS, 2 * CAP, FFW // 2), SHARE, split_axis=0, concat_axis=0, tiled=True
    ).reshape(COUNT, FFW // 2)

    grads, grad_probs = pl.pallas_call(
        finish,
        out_shape=(
            jax.ShapeDtypeStruct((tokens, 2 * FFW), jnp.bfloat16),
            jax.ShapeDtypeStruct((1, tokens), jnp.bfloat16),
        ),
        in_specs=[pl.BlockSpec(memory_space=pltpu.VMEM)] * 4,
        out_specs=(pl.BlockSpec(memory_space=pltpu.VMEM),) * 2,
        compiler_params=pltpu.CompilerParams(vmem_limit_bytes=20 * 2**20),
        cost_estimate=pl.CostEstimate(flops=2 * 10**8, bytes_accessed=2 * 10**6, transcendentals=10**5),
    )(came, gate_up.reshape(tokens, 2 * FFW), route_probs.reshape(1, tokens), first.reshape(1, tokens))
    return grads.reshape(tokens, 1, 2 * FFW), grad_probs.reshape(tokens, 1)


def solution(mesh):
    named = Mesh(mesh.devices.reshape(2, 8, 8, 4, 2), AXES)
    return jax.shard_map(
        body,
        mesh=named,
        in_specs=(
            P(AXES, None),
            P(AXES, None, None),
            P(AXES, None),
            P(AXES, None),
            P(("xh", "core"), ("xl", "y", "z"), None),
        ),
        out_specs=(P(AXES, None, None), P(AXES, None)),
        check_vma=False,
    )
```

```python
import jax
import jax.numpy as jnp
from jax import lax
from jax.experimental import pallas as pl
from jax.experimental.pallas import tpu as pltpu
from jax.sharding import Mesh, PartitionSpec as P

D = 4096
FFW = 768
HALF = D // 2
QUART = D // 4
EXPERTS = 8
CAP = 20
PEERS = 16

AXES = ("xl", "y", "z", "xh", "core")
SHARE = ("xl", "xh", "core")

TORUS = ("y", "z", "xh", "core")
RING = 8
HALF_RING = RING // 2
LINES = [(h, c) for h in range(4) for c in range(2)]
COUNT = PEERS * 2 * CAP


def place_of(y, z, h, c):
    return (((y % RING) * RING + z % RING) * 4 + h) * 2 + c


def first_groups():
    return [
        [place_of(k, i, h, c) if c == 0 else place_of(i, k, h, c) for i in range(RING)]
        for h, c in LINES
        for k in range(RING)
    ]


def second_shift(step):
    return [
        (place_of(y, z, h, c), place_of(y + step, z, h, c) if c == 0 else place_of(y, z + step, h, c))
        for y in range(RING)
        for z in range(RING)
        for h, c in LINES
    ]


PIECES = (
    (0, 0, RING, 0, 0),
    (1, 0, RING, 3, 0),
    (2, 0, RING, -3, 0),
    (3, 0, RING, -1, 0),
    (3, RING, RING, 2, 0),
    (3, 2 * RING, HALF_RING, 4, 0),
    (4, 0, RING, 1, 0),
    (4, RING, RING, -2, 0),
    (4, 2 * RING, HALF_RING, 4, HALF_RING),
)
ARRAYS = 5


def product(rows_ref, *refs):
    parts, out_ref, weight_ref = refs[:ARRAYS], refs[ARRAYS], refs[ARRAYS + 1]
    y, z, core = lax.axis_index("y"), lax.axis_index("z"), lax.axis_index("core")
    mine = jnp.where(core == 0, y, z)
    outer = jnp.where(core == 0, RING, 1)
    inner = jnp.where(core == 0, 1, RING)
    for which, first, blocks, offset, at in PIECES:
        source = lax.rem(mine + offset + RING, RING)
        for i in range(blocks):
            weight_ref[source * outer + (at + i) * inner] = parts[which][first + i]

    half = RING * RING // 2
    width = weight_ref.shape[1] * half
    back = jnp.dot(
        rows_ref[: COUNT // 2], weight_ref[:half].reshape(width, FFW), preferred_element_type=jnp.float32
    ) + jnp.dot(
        rows_ref[COUNT // 2 :], weight_ref[half:].reshape(width, FFW), preferred_element_type=jnp.float32
    )
    back = back.astype(jnp.bfloat16)
    back = jnp.concatenate([back[:, : FFW // 2], back[:, FFW // 2 :]], axis=0)

    i = lax.broadcasted_iota(jnp.int32, (1, COUNT), 1)
    piece = (i >= COUNT // 2).astype(jnp.int32)
    j = i - piece * (COUNT // 2)
    source = (j * 3277) >> 16
    order = source * (2 * CAP) + piece * CAP + j - source * CAP
    give = (lax.broadcasted_iota(jnp.int32, (COUNT, COUNT), 0) == order).astype(jnp.bfloat16)
    out_ref[...] = jnp.dot(give, back, preferred_element_type=jnp.float32).astype(jnp.bfloat16)


def join(line_ref, ahead_ref, behind_ref, up_ref, down_ref):
    up_ref[:RING] = line_ref[...]
    up_ref[RING : 2 * RING] = ahead_ref[...]
    up_ref[2 * RING :] = behind_ref[:HALF_RING]
    down_ref[:RING] = line_ref[...]
    down_ref[RING : 2 * RING] = behind_ref[...]
    down_ref[2 * RING :] = ahead_ref[HALF_RING:]


def finish(came_ref, pre_ref, probs_ref, first_ref, grads_ref, grad_probs_ref):
    tokens = pre_ref.shape[0]
    square = (tokens, tokens)
    line = lax.broadcasted_iota(jnp.int32, square, 0)
    told = jnp.where(line == 0, first_ref[...].astype(jnp.float32), probs_ref[...].astype(jnp.float32)).T
    first, prob = told[:, :1].astype(jnp.int32), told[:, 1:2]
    place = lax.broadcasted_iota(jnp.int32, (tokens, COUNT), 1)
    place = jnp.where(place >= COUNT // 2, place - COUNT // 2, place)
    total = jnp.zeros((tokens, 1), jnp.float32)
    part = FFW // 2
    for c in range(2):
        back = jnp.dot(
            (place == first + c * CAP).astype(jnp.bfloat16), came_ref[...], preferred_element_type=jnp.float32
        )
        gate = pre_ref[:, c * part : (c + 1) * part].astype(jnp.float32)
        up = pre_ref[:, FFW + c * part : FFW + (c + 1) * part].astype(jnp.float32)
        squash = 1.0 / (1.0 + jnp.exp(-gate))
        silu = gate * squash
        hidden = (silu * up).astype(jnp.bfloat16).astype(jnp.float32)
        total += jnp.sum(hidden * back, axis=1, keepdims=True)
        scaled = prob * back
        grads_ref[:, c * part : (c + 1) * part] = (
            scaled * up * squash * (1.0 + gate * (1.0 - squash))
        ).astype(jnp.bfloat16)
        grads_ref[:, FFW + c * part : FFW + (c + 1) * part] = (scaled * silu).astype(jnp.bfloat16)
    grad_probs_ref[...] = jnp.broadcast_to(total, square).T[:1].astype(jnp.bfloat16)


def onehot(index, rows):
    return (jnp.arange(rows, dtype=jnp.int32)[:, None] == index[None, :]).astype(jnp.bfloat16)


def body(cotangent, gate_up, route_probs, routes, down_weight):
    tokens = cotangent.shape[0]

    own = down_weight[0]
    line = lax.all_to_all(
        jnp.broadcast_to(own[None], (RING,) + own.shape),
        TORUS,
        split_axis=0,
        concat_axis=0,
        axis_index_groups=first_groups(),
        tiled=True,
    )
    ahead = lax.ppermute(line, TORUS, second_shift(-3))
    behind = lax.ppermute(line, TORUS, second_shift(3))
    passed = jax.ShapeDtypeStruct((2 * RING + HALF_RING,) + own.shape, jnp.bfloat16)
    up, down = pl.pallas_call(
        join,
        out_shape=(passed, passed),
        in_specs=[pl.BlockSpec(memory_space=pltpu.VMEM)] * 3,
        out_specs=(pl.BlockSpec(memory_space=pltpu.VMEM),) * 2,
        compiler_params=pltpu.CompilerParams(vmem_limit_bytes=16 * 2**20),
        cost_estimate=pl.CostEstimate(flops=2 * 10**11, bytes_accessed=4 * 10**6, transcendentals=0),
    )(line, ahead, behind)
    parts = [line, ahead, behind, lax.ppermute(up, TORUS, second_shift(1)), lax.ppermute(down, TORUS, second_shift(-1))]

    flat_routes = routes.reshape(tokens)
    member = (flat_routes[:, None] == jnp.arange(EXPERTS, dtype=jnp.int32)[None, :]).astype(jnp.int32)
    rank = jnp.sum(jnp.cumsum(member, axis=0) * member, axis=1) - 1
    first = flat_routes * (2 * CAP) + rank
    both = jnp.concatenate([first, first + CAP])
    placing = onehot(both, EXPERTS * 2 * CAP)
    quarters = [cotangent[:, i * QUART : (i + 1) * QUART] for i in range(4)]
    sent = jnp.stack(
        [
            jnp.dot(
                placing,
                jnp.concatenate([quarters[2 * h], quarters[2 * h + 1]], axis=0),
                preferred_element_type=jnp.float32,
            ).astype(jnp.bfloat16)
            for h in range(2)
        ]
    ).reshape(PEERS, 2 * CAP, QUART)
    got = lax.all_to_all(sent, SHARE, split_axis=0, concat_axis=0, tiled=True)

    order = jnp.arange(COUNT, dtype=jnp.int32)
    order = (order % (COUNT // 2)) // CAP * (2 * CAP) + order // (COUNT // 2) * CAP + order % CAP
    take = (order[:, None] == jnp.arange(COUNT, dtype=jnp.int32)[None, :]).astype(jnp.bfloat16)
    rows = jnp.dot(take, got.reshape(COUNT, QUART), preferred_element_type=jnp.float32).astype(jnp.bfloat16)
    back = pl.pallas_call(
        product,
        out_shape=jax.ShapeDtypeStruct((COUNT, FFW // 2), jnp.bfloat16),
        in_specs=[pl.BlockSpec(memory_space=pltpu.VMEM)] * (ARRAYS + 1),
        out_specs=pl.BlockSpec(memory_space=pltpu.VMEM),
        scratch_shapes=[pltpu.VMEM((RING * RING,) + own.shape, jnp.bfloat16)],
        compiler_params=pltpu.CompilerParams(vmem_limit_bytes=20 * 2**20),
        cost_estimate=pl.CostEstimate(flops=2 * 10**9, bytes_accessed=10**7, transcendentals=0),
    )(rows, *parts)
    came = lax.all_to_all(
        back.reshape(PEERS, 2 * CAP, FFW // 2), SHARE, split_axis=0, concat_axis=0, tiled=True
    ).reshape(COUNT, FFW // 2)

    grads, grad_probs = pl.pallas_call(
        finish,
        out_shape=(
            jax.ShapeDtypeStruct((tokens, 2 * FFW), jnp.bfloat16),
            jax.ShapeDtypeStruct((1, tokens), jnp.bfloat16),
        ),
        in_specs=[pl.BlockSpec(memory_space=pltpu.VMEM)] * 4,
        out_specs=(pl.BlockSpec(memory_space=pltpu.VMEM),) * 2,
        compiler_params=pltpu.CompilerParams(vmem_limit_bytes=20 * 2**20),
        cost_estimate=pl.CostEstimate(flops=2 * 10**8, bytes_accessed=2 * 10**6, transcendentals=10**5),
    )(came, gate_up.reshape(tokens, 2 * FFW), route_probs.reshape(1, tokens), first.reshape(1, tokens))
    return grads.reshape(tokens, 1, 2 * FFW), grad_probs.reshape(tokens, 1)


def solution(mesh):
    named = Mesh(mesh.devices.reshape(2, 8, 8, 4, 2), AXES)
    return jax.shard_map(
        body,
        mesh=named,
        in_specs=(
            P(AXES, None),
            P(AXES, None, None),
            P(AXES, None),
            P(AXES, None),
            P(("xh", "core"), ("xl", "y", "z"), None),
        ),
        out_specs=(P(AXES, None, None), P(AXES, None)),
        check_vma=False,
    )
```

```python
import jax
import jax.numpy as jnp
from jax import lax
from jax.experimental import pallas as pl
from jax.experimental.pallas import tpu as pltpu
from jax.sharding import Mesh, PartitionSpec as P

D = 4096
FFW = 768
HALF = D // 2
QUART = D // 4
EXPERTS = 8
CAP = 20
PEERS = 16

AXES = ("xl", "y", "z", "xh", "core")
SHARE = ("xl", "xh", "core")

TORUS = ("y", "z", "xh", "core")
RING = 8
HALF_RING = RING // 2
LINES = [(h, c) for h in range(4) for c in range(2)]
COUNT = PEERS * 2 * CAP


def place_of(y, z, h, c):
    return (((y % RING) * RING + z % RING) * 4 + h) * 2 + c


def first_groups():
    return [
        [place_of(k, i, h, c) if c == 0 else place_of(i, k, h, c) for i in range(RING)]
        for h, c in LINES
        for k in range(RING)
    ]


def second_shift(step):
    return [
        (place_of(y, z, h, c), place_of(y + step, z, h, c) if c == 0 else place_of(y, z + step, h, c))
        for y in range(RING)
        for z in range(RING)
        for h, c in LINES
    ]


PIECES = (
    (0, 0, RING, 0, 0),
    (1, 0, RING, 3, 0),
    (2, 0, RING, -3, 0),
    (3, 0, RING, -1, 0),
    (3, RING, RING, 2, 0),
    (3, 2 * RING, HALF_RING, 4, 0),
    (4, 0, RING, 1, 0),
    (4, RING, RING, -2, 0),
    (4, 2 * RING, HALF_RING, 4, HALF_RING),
)
ARRAYS = 5


def product(got_ref, *refs):
    parts, out_ref, weight_ref = refs[:ARRAYS], refs[ARRAYS], refs[ARRAYS + 1]
    y, z, core = lax.axis_index("y"), lax.axis_index("z"), lax.axis_index("core")
    mine = jnp.where(core == 0, y, z)
    outer = jnp.where(core == 0, RING, 1)
    inner = jnp.where(core == 0, 1, RING)
    for which, first, blocks, offset, at in PIECES:
        source = lax.rem(mine + offset + RING, RING)
        for i in range(blocks):
            weight_ref[source * outer + (at + i) * inner] = parts[which][first + i]

    def order(shape, axis):
        i = lax.broadcasted_iota(jnp.int32, shape, axis)
        piece = (i >= COUNT // 2).astype(jnp.int32)
        j = i - piece * (COUNT // 2)
        source = (j * 3277) >> 16
        return source * (2 * CAP) + piece * CAP + j - source * CAP

    take = (lax.broadcasted_iota(jnp.int32, (COUNT, COUNT), 1) == order((COUNT, 1), 0)).astype(jnp.bfloat16)
    rows = jnp.dot(take, got_ref[...], preferred_element_type=jnp.float32).astype(jnp.bfloat16)
    half = RING * RING // 2
    width = weight_ref.shape[1] * half
    back = jnp.dot(
        rows[: COUNT // 2], weight_ref[:half].reshape(width, FFW), preferred_element_type=jnp.float32
    ) + jnp.dot(
        rows[COUNT // 2 :], weight_ref[half:].reshape(width, FFW), preferred_element_type=jnp.float32
    )
    back = back.astype(jnp.bfloat16)
    back = jnp.concatenate([back[:, : FFW // 2], back[:, FFW // 2 :]], axis=0)

    give = (lax.broadcasted_iota(jnp.int32, (COUNT, COUNT), 0) == order((1, COUNT), 1)).astype(jnp.bfloat16)
    out_ref[...] = jnp.dot(give, back, preferred_element_type=jnp.float32).astype(jnp.bfloat16)


def join(line_ref, ahead_ref, behind_ref, up_ref, down_ref):
    up_ref[:RING] = line_ref[...]
    up_ref[RING : 2 * RING] = ahead_ref[...]
    up_ref[2 * RING :] = behind_ref[:HALF_RING]
    down_ref[:RING] = line_ref[...]
    down_ref[RING : 2 * RING] = behind_ref[...]
    down_ref[2 * RING :] = ahead_ref[HALF_RING:]


def finish(came_ref, pre_ref, probs_ref, first_ref, grads_ref, grad_probs_ref):
    tokens = pre_ref.shape[0]
    square = (tokens, tokens)
    line = lax.broadcasted_iota(jnp.int32, square, 0)
    told = jnp.where(line == 0, first_ref[...].astype(jnp.float32), probs_ref[...].astype(jnp.float32)).T
    first, prob = told[:, :1].astype(jnp.int32), told[:, 1:2]
    place = lax.broadcasted_iota(jnp.int32, (tokens, COUNT), 1)
    place = jnp.where(place >= COUNT // 2, place - COUNT // 2, place)
    total = jnp.zeros((tokens, 1), jnp.float32)
    part = FFW // 2
    for c in range(2):
        back = jnp.dot(
            (place == first + c * CAP).astype(jnp.bfloat16), came_ref[...], preferred_element_type=jnp.float32
        )
        gate = pre_ref[:, c * part : (c + 1) * part].astype(jnp.float32)
        up = pre_ref[:, FFW + c * part : FFW + (c + 1) * part].astype(jnp.float32)
        squash = 1.0 / (1.0 + jnp.exp(-gate))
        silu = gate * squash
        hidden = (silu * up).astype(jnp.bfloat16).astype(jnp.float32)
        total += jnp.sum(hidden * back, axis=1, keepdims=True)
        scaled = prob * back
        grads_ref[:, c * part : (c + 1) * part] = (
            scaled * up * squash * (1.0 + gate * (1.0 - squash))
        ).astype(jnp.bfloat16)
        grads_ref[:, FFW + c * part : FFW + (c + 1) * part] = (scaled * silu).astype(jnp.bfloat16)
    grad_probs_ref[...] = jnp.broadcast_to(total, square).T[:1].astype(jnp.bfloat16)


def onehot(index, rows):
    return (jnp.arange(rows, dtype=jnp.int32)[:, None] == index[None, :]).astype(jnp.bfloat16)


def body(cotangent, gate_up, route_probs, routes, down_weight):
    tokens = cotangent.shape[0]

    own = down_weight[0]
    line = lax.all_to_all(
        jnp.broadcast_to(own[None], (RING,) + own.shape),
        TORUS,
        split_axis=0,
        concat_axis=0,
        axis_index_groups=first_groups(),
        tiled=True,
    )

    flat_routes = routes.reshape(tokens)
    member = (flat_routes[:, None] == jnp.arange(EXPERTS, dtype=jnp.int32)[None, :]).astype(jnp.int32)
    rank = jnp.sum(jnp.cumsum(member, axis=0) * member, axis=1) - 1
    first = flat_routes * (2 * CAP) + rank
    both = jnp.concatenate([first, first + CAP])
    placing = onehot(both, EXPERTS * 2 * CAP)
    quarters = [cotangent[:, i * QUART : (i + 1) * QUART] for i in range(4)]
    sent = jnp.stack(
        [
            jnp.dot(
                placing,
                jnp.concatenate([quarters[2 * h], quarters[2 * h + 1]], axis=0),
                preferred_element_type=jnp.float32,
            ).astype(jnp.bfloat16)
            for h in range(2)
        ]
    ).reshape(PEERS, 2 * CAP, QUART)
    line, sent = lax.optimization_barrier((line, sent))
    ahead = lax.ppermute(line, TORUS, second_shift(-3))
    behind = lax.ppermute(line, TORUS, second_shift(3))
    passed = jax.ShapeDtypeStruct((2 * RING + HALF_RING,) + own.shape, jnp.bfloat16)
    up, down = pl.pallas_call(
        join,
        out_shape=(passed, passed),
        in_specs=[pl.BlockSpec(memory_space=pltpu.VMEM)] * 3,
        out_specs=(pl.BlockSpec(memory_space=pltpu.VMEM),) * 2,
        compiler_params=pltpu.CompilerParams(vmem_limit_bytes=16 * 2**20),
        cost_estimate=pl.CostEstimate(flops=2 * 10**11, bytes_accessed=4 * 10**6, transcendentals=0),
    )(line, ahead, behind)
    parts = [line, ahead, behind, lax.ppermute(up, TORUS, second_shift(1)), lax.ppermute(down, TORUS, second_shift(-1))]
    got = lax.all_to_all(sent, SHARE, split_axis=0, concat_axis=0, tiled=True)

    back = pl.pallas_call(
        product,
        out_shape=jax.ShapeDtypeStruct((COUNT, FFW // 2), jnp.bfloat16),
        in_specs=[pl.BlockSpec(memory_space=pltpu.VMEM)] * (ARRAYS + 1),
        out_specs=pl.BlockSpec(memory_space=pltpu.VMEM),
        scratch_shapes=[pltpu.VMEM((RING * RING,) + own.shape, jnp.bfloat16)],
        compiler_params=pltpu.CompilerParams(vmem_limit_bytes=20 * 2**20),
        cost_estimate=pl.CostEstimate(flops=2 * 10**9, bytes_accessed=10**7, transcendentals=0),
    )(got.reshape(COUNT, QUART), *parts)
    came = lax.all_to_all(
        back.reshape(PEERS, 2 * CAP, FFW // 2), SHARE, split_axis=0, concat_axis=0, tiled=True
    ).reshape(COUNT, FFW // 2)

    grads, grad_probs = pl.pallas_call(
        finish,
        out_shape=(
            jax.ShapeDtypeStruct((tokens, 2 * FFW), jnp.bfloat16),
            jax.ShapeDtypeStruct((1, tokens), jnp.bfloat16),
        ),
        in_specs=[pl.BlockSpec(memory_space=pltpu.VMEM)] * 4,
        out_specs=(pl.BlockSpec(memory_space=pltpu.VMEM),) * 2,
        compiler_params=pltpu.CompilerParams(vmem_limit_bytes=20 * 2**20),
        cost_estimate=pl.CostEstimate(flops=2 * 10**8, bytes_accessed=2 * 10**6, transcendentals=10**5),
    )(came, gate_up.reshape(tokens, 2 * FFW), route_probs.reshape(1, tokens), first.reshape(1, tokens))
    return grads.reshape(tokens, 1, 2 * FFW), grad_probs.reshape(tokens, 1)


def solution(mesh):
    named = Mesh(mesh.devices.reshape(2, 8, 8, 4, 2), AXES)
    return jax.shard_map(
        body,
        mesh=named,
        in_specs=(
            P(AXES, None),
            P(AXES, None, None),
            P(AXES, None),
            P(AXES, None),
            P(("xh", "core"), ("xl", "y", "z"), None),
        ),
        out_specs=(P(AXES, None, None), P(AXES, None)),
        check_vma=False,
    )
```

```python
import jax
import jax.numpy as jnp
from jax import lax
from jax.experimental import pallas as pl
from jax.experimental.pallas import tpu as pltpu
from jax.sharding import Mesh, PartitionSpec as P

D = 4096
FFW = 768
HALF = D // 2
QUART = D // 4
EXPERTS = 8
CAP = 20
PEERS = 16

AXES = ("xl", "y", "z", "xh", "core")
SHARE = ("xl", "xh", "core")

TORUS = ("y", "z", "xh", "core")
RING = 8
HALF_RING = RING // 2
LINES = [(h, c) for h in range(4) for c in range(2)]
COUNT = PEERS * 2 * CAP


def place_of(y, z, h, c):
    return (((y % RING) * RING + z % RING) * 4 + h) * 2 + c


def first_groups():
    return [
        [place_of(k, i, h, c) if c == 0 else place_of(i, k, h, c) for i in range(RING)]
        for h, c in LINES
        for k in range(RING)
    ]


def second_shift(step):
    return [
        (place_of(y, z, h, c), place_of(y + step, z, h, c) if c == 0 else place_of(y, z + step, h, c))
        for y in range(RING)
        for z in range(RING)
        for h, c in LINES
    ]


PIECES = (
    (0, 0, RING, 0, 0),
    (1, 0, RING, 3, 0),
    (2, 0, RING, -3, 0),
    (3, 0, RING, -1, 0),
    (3, RING, RING, 2, 0),
    (3, 2 * RING, HALF_RING, 4, 0),
    (4, 0, RING, 1, 0),
    (4, RING, RING, -2, 0),
    (4, 2 * RING, HALF_RING, 4, HALF_RING),
)
ARRAYS = 5


def product(got_ref, *refs):
    parts, out_ref, weight_ref, held_ref, rows_ref, sem = refs[:ARRAYS], refs[ARRAYS], *refs[ARRAYS + 1 :]
    fetch = pltpu.make_async_copy(got_ref, held_ref, sem)
    fetch.start()
    y, z, core = lax.axis_index("y"), lax.axis_index("z"), lax.axis_index("core")
    mine = jnp.where(core == 0, y, z)
    outer = jnp.where(core == 0, RING, 1)
    inner = jnp.where(core == 0, 1, RING)
    for which, first, blocks, offset, at in PIECES:
        source = lax.rem(mine + offset + RING, RING)
        for i in range(blocks):
            weight_ref[source * outer + (at + i) * inner] = parts[which][first + i]

    def order(shape, axis):
        i = lax.broadcasted_iota(jnp.int32, shape, axis)
        piece = (i >= COUNT // 2).astype(jnp.int32)
        j = i - piece * (COUNT // 2)
        source = (j * 3277) >> 16
        return source * (2 * CAP) + piece * CAP + j - source * CAP

    take = (lax.broadcasted_iota(jnp.int32, (COUNT, COUNT), 1) == order((COUNT, 1), 0)).astype(jnp.bfloat16)
    fetch.wait()
    tile = QUART // 4
    for k in range(4):
        rows_ref[:, k * tile : (k + 1) * tile] = jnp.dot(
            take, held_ref[:, k * tile : (k + 1) * tile], preferred_element_type=jnp.float32
        ).astype(jnp.bfloat16)
    half = RING * RING // 2
    width = weight_ref.shape[1] * half
    back = jnp.dot(
        rows_ref[: COUNT // 2], weight_ref[:half].reshape(width, FFW), preferred_element_type=jnp.float32
    ) + jnp.dot(
        rows_ref[COUNT // 2 :], weight_ref[half:].reshape(width, FFW), preferred_element_type=jnp.float32
    )
    back = back.astype(jnp.bfloat16)
    back = jnp.concatenate([back[:, : FFW // 2], back[:, FFW // 2 :]], axis=0)

    give = (lax.broadcasted_iota(jnp.int32, (COUNT, COUNT), 0) == order((1, COUNT), 1)).astype(jnp.bfloat16)
    out_ref[...] = jnp.dot(give, back, preferred_element_type=jnp.float32).astype(jnp.bfloat16)


def join(line_ref, ahead_ref, behind_ref, up_ref, down_ref):
    up_ref[:RING] = line_ref[...]
    up_ref[RING : 2 * RING] = ahead_ref[...]
    up_ref[2 * RING :] = behind_ref[:HALF_RING]
    down_ref[:RING] = line_ref[...]
    down_ref[RING : 2 * RING] = behind_ref[...]
    down_ref[2 * RING :] = ahead_ref[HALF_RING:]


def finish(came_ref, pre_ref, probs_ref, first_ref, grads_ref, grad_probs_ref):
    tokens = pre_ref.shape[0]
    square = (tokens, tokens)
    line = lax.broadcasted_iota(jnp.int32, square, 0)
    told = jnp.where(line == 0, first_ref[...].astype(jnp.float32), probs_ref[...].astype(jnp.float32)).T
    first, prob = told[:, :1].astype(jnp.int32), told[:, 1:2]
    place = lax.broadcasted_iota(jnp.int32, (tokens, COUNT), 1)
    place = jnp.where(place >= COUNT // 2, place - COUNT // 2, place)
    total = jnp.zeros((tokens, 1), jnp.float32)
    part = FFW // 2
    for c in range(2):
        back = jnp.dot(
            (place == first + c * CAP).astype(jnp.bfloat16), came_ref[...], preferred_element_type=jnp.float32
        )
        gate = pre_ref[:, c * part : (c + 1) * part].astype(jnp.float32)
        up = pre_ref[:, FFW + c * part : FFW + (c + 1) * part].astype(jnp.float32)
        squash = 1.0 / (1.0 + jnp.exp(-gate))
        silu = gate * squash
        hidden = (silu * up).astype(jnp.bfloat16).astype(jnp.float32)
        total += jnp.sum(hidden * back, axis=1, keepdims=True)
        scaled = prob * back
        grads_ref[:, c * part : (c + 1) * part] = (
            scaled * up * squash * (1.0 + gate * (1.0 - squash))
        ).astype(jnp.bfloat16)
        grads_ref[:, FFW + c * part : FFW + (c + 1) * part] = (scaled * silu).astype(jnp.bfloat16)
    grad_probs_ref[...] = jnp.broadcast_to(total, square).T[:1].astype(jnp.bfloat16)


def onehot(index, rows):
    return (jnp.arange(rows, dtype=jnp.int32)[:, None] == index[None, :]).astype(jnp.bfloat16)


def body(cotangent, gate_up, route_probs, routes, down_weight):
    tokens = cotangent.shape[0]

    own = down_weight[0]
    line = lax.all_to_all(
        jnp.broadcast_to(own[None], (RING,) + own.shape),
        TORUS,
        split_axis=0,
        concat_axis=0,
        axis_index_groups=first_groups(),
        tiled=True,
    )

    flat_routes = routes.reshape(tokens)
    member = (flat_routes[:, None] == jnp.arange(EXPERTS, dtype=jnp.int32)[None, :]).astype(jnp.int32)
    rank = jnp.sum(jnp.cumsum(member, axis=0) * member, axis=1) - 1
    first = flat_routes * (2 * CAP) + rank
    both = jnp.concatenate([first, first + CAP])
    placing = onehot(both, EXPERTS * 2 * CAP)
    quarters = [cotangent[:, i * QUART : (i + 1) * QUART] for i in range(4)]
    sent = jnp.stack(
        [
            jnp.dot(
                placing,
                jnp.concatenate([quarters[2 * h], quarters[2 * h + 1]], axis=0),
                preferred_element_type=jnp.float32,
            ).astype(jnp.bfloat16)
            for h in range(2)
        ]
    ).reshape(PEERS, 2 * CAP, QUART)
    line, sent = lax.optimization_barrier((line, sent))
    ahead = lax.ppermute(line, TORUS, second_shift(-3))
    behind = lax.ppermute(line, TORUS, second_shift(3))
    passed = jax.ShapeDtypeStruct((2 * RING + HALF_RING,) + own.shape, jnp.bfloat16)
    up, down = pl.pallas_call(
        join,
        out_shape=(passed, passed),
        in_specs=[pl.BlockSpec(memory_space=pltpu.VMEM)] * 3,
        out_specs=(pl.BlockSpec(memory_space=pltpu.VMEM),) * 2,
        compiler_params=pltpu.CompilerParams(vmem_limit_bytes=16 * 2**20),
        cost_estimate=pl.CostEstimate(flops=2 * 10**11, bytes_accessed=4 * 10**6, transcendentals=0),
    )(line, ahead, behind)
    parts = [line, ahead, behind, lax.ppermute(up, TORUS, second_shift(1)), lax.ppermute(down, TORUS, second_shift(-1))]
    got = lax.all_to_all(sent, SHARE, split_axis=0, concat_axis=0, tiled=True)

    back = pl.pallas_call(
        product,
        out_shape=jax.ShapeDtypeStruct((COUNT, FFW // 2), jnp.bfloat16),
        in_specs=[pl.BlockSpec(memory_space=pl.ANY)] + [pl.BlockSpec(memory_space=pltpu.VMEM)] * ARRAYS,
        out_specs=pl.BlockSpec(memory_space=pltpu.VMEM),
        scratch_shapes=[
            pltpu.VMEM((RING * RING,) + own.shape, jnp.bfloat16),
            pltpu.VMEM((COUNT, QUART), jnp.bfloat16),
            pltpu.VMEM((COUNT, QUART), jnp.bfloat16),
            pltpu.SemaphoreType.DMA,
        ],
        compiler_params=pltpu.CompilerParams(vmem_limit_bytes=20 * 2**20),
        cost_estimate=pl.CostEstimate(flops=2 * 10**9, bytes_accessed=10**7, transcendentals=0),
    )(got.reshape(COUNT, QUART), *parts)
    came = lax.all_to_all(
        back.reshape(PEERS, 2 * CAP, FFW // 2), SHARE, split_axis=0, concat_axis=0, tiled=True
    ).reshape(COUNT, FFW // 2)

    grads, grad_probs = pl.pallas_call(
        finish,
        out_shape=(
            jax.ShapeDtypeStruct((tokens, 2 * FFW), jnp.bfloat16),
            jax.ShapeDtypeStruct((1, tokens), jnp.bfloat16),
        ),
        in_specs=[pl.BlockSpec(memory_space=pltpu.VMEM)] * 4,
        out_specs=(pl.BlockSpec(memory_space=pltpu.VMEM),) * 2,
        compiler_params=pltpu.CompilerParams(vmem_limit_bytes=20 * 2**20),
        cost_estimate=pl.CostEstimate(flops=2 * 10**8, bytes_accessed=2 * 10**6, transcendentals=10**5),
    )(came, gate_up.reshape(tokens, 2 * FFW), route_probs.reshape(1, tokens), first.reshape(1, tokens))
    return grads.reshape(tokens, 1, 2 * FFW), grad_probs.reshape(tokens, 1)


def solution(mesh):
    named = Mesh(mesh.devices.reshape(2, 8, 8, 4, 2), AXES)
    return jax.shard_map(
        body,
        mesh=named,
        in_specs=(
            P(AXES, None),
            P(AXES, None, None),
            P(AXES, None),
            P(AXES, None),
            P(("xh", "core"), ("xl", "y", "z"), None),
        ),
        out_specs=(P(AXES, None, None), P(AXES, None)),
        check_vma=False,
    )
```

```python
import jax
import jax.numpy as jnp
from jax import lax
from jax.experimental import pallas as pl
from jax.experimental.pallas import tpu as pltpu
from jax.sharding import Mesh, PartitionSpec as P

D = 4096
FFW = 768
HALF = D // 2
QUART = D // 4
EXPERTS = 8
CAP = 20
PEERS = 16

AXES = ("xl", "y", "z", "xh", "core")
SHARE = ("xl", "xh", "core")

TORUS = ("y", "z", "xh", "core")
RING = 8
HALF_RING = RING // 2
LINES = [(h, c) for h in range(4) for c in range(2)]
COUNT = PEERS * 2 * CAP


def place_of(y, z, h, c):
    return (((y % RING) * RING + z % RING) * 4 + h) * 2 + c


def first_groups():
    return [
        [place_of(k, i, h, c) if c == 0 else place_of(i, k, h, c) for i in range(RING)]
        for h, c in LINES
        for k in range(RING)
    ]


def second_shift(step):
    return [
        (place_of(y, z, h, c), place_of(y + step, z, h, c) if c == 0 else place_of(y, z + step, h, c))
        for y in range(RING)
        for z in range(RING)
        for h, c in LINES
    ]


PIECES = (
    (0, 0, RING, 0, 0),
    (1, 0, RING, 3, 0),
    (2, 0, RING, -3, 0),
    (3, 0, RING, -1, 0),
    (3, RING, RING, 2, 0),
    (3, 2 * RING, HALF_RING, 4, 0),
    (4, 0, RING, 1, 0),
    (4, RING, RING, -2, 0),
    (4, 2 * RING, HALF_RING, 4, HALF_RING),
)
ARRAYS = 5


def product(got_ref, *refs):
    parts, out_ref, weight_ref, held_ref, rows_ref, sem = refs[:ARRAYS], refs[ARRAYS], *refs[ARRAYS + 1 :]
    fetch = pltpu.make_async_copy(got_ref, held_ref, sem)
    fetch.start()
    y, z, core = lax.axis_index("y"), lax.axis_index("z"), lax.axis_index("core")
    mine = jnp.where(core == 0, y, z)
    outer = jnp.where(core == 0, RING, 1)
    inner = jnp.where(core == 0, 1, RING)
    for which, first, blocks, offset, at in PIECES:
        source = lax.rem(mine + offset + RING, RING)
        for i in range(blocks):
            weight_ref[source * outer + (at + i) * inner] = parts[which][first + i]

    def order(shape, axis):
        i = lax.broadcasted_iota(jnp.int32, shape, axis)
        piece = (i >= COUNT // 2).astype(jnp.int32)
        j = i - piece * (COUNT // 2)
        source = (j * 3277) >> 16
        return source * (2 * CAP) + piece * CAP + j - source * CAP

    take = (lax.broadcasted_iota(jnp.int32, (COUNT, COUNT), 1) == order((COUNT, 1), 0)).astype(jnp.bfloat16)
    fetch.wait()
    tile = QUART // 4
    for k in range(4):
        rows_ref[:, k * tile : (k + 1) * tile] = jnp.dot(
            take, held_ref[:, k * tile : (k + 1) * tile], preferred_element_type=jnp.float32
        ).astype(jnp.bfloat16)
    half = RING * RING // 2
    width = weight_ref.shape[1] * half
    back = jnp.dot(
        rows_ref[: COUNT // 2], weight_ref[:half].reshape(width, FFW), preferred_element_type=jnp.float32
    ) + jnp.dot(
        rows_ref[COUNT // 2 :], weight_ref[half:].reshape(width, FFW), preferred_element_type=jnp.float32
    )
    back = back.astype(jnp.bfloat16)
    back = jnp.concatenate([back[:, : FFW // 2], back[:, FFW // 2 :]], axis=0)

    give = (lax.broadcasted_iota(jnp.int32, (COUNT, COUNT), 0) == order((1, COUNT), 1)).astype(jnp.bfloat16)
    out_ref[...] = jnp.dot(give, back, preferred_element_type=jnp.float32).astype(jnp.bfloat16)


def spread(own_ref, out_ref):
    for i in range(RING):
        out_ref[i] = own_ref[...]


def join(line_ref, ahead_ref, behind_ref, up_ref, down_ref):
    up_ref[:RING] = line_ref[...]
    up_ref[RING : 2 * RING] = ahead_ref[...]
    up_ref[2 * RING :] = behind_ref[:HALF_RING]
    down_ref[:RING] = line_ref[...]
    down_ref[RING : 2 * RING] = behind_ref[...]
    down_ref[2 * RING :] = ahead_ref[HALF_RING:]


def finish(came_ref, pre_ref, probs_ref, first_ref, grads_ref, grad_probs_ref):
    tokens = pre_ref.shape[0]
    square = (tokens, tokens)
    line = lax.broadcasted_iota(jnp.int32, square, 0)
    told = jnp.where(line == 0, first_ref[...].astype(jnp.float32), probs_ref[...].astype(jnp.float32)).T
    first, prob = told[:, :1].astype(jnp.int32), told[:, 1:2]
    place = lax.broadcasted_iota(jnp.int32, (tokens, COUNT), 1)
    place = jnp.where(place >= COUNT // 2, place - COUNT // 2, place)
    total = jnp.zeros((tokens, 1), jnp.float32)
    part = FFW // 2
    for c in range(2):
        back = jnp.dot(
            (place == first + c * CAP).astype(jnp.bfloat16), came_ref[...], preferred_element_type=jnp.float32
        )
        gate = pre_ref[:, c * part : (c + 1) * part].astype(jnp.float32)
        up = pre_ref[:, FFW + c * part : FFW + (c + 1) * part].astype(jnp.float32)
        squash = 1.0 / (1.0 + jnp.exp(-gate))
        silu = gate * squash
        hidden = (silu * up).astype(jnp.bfloat16).astype(jnp.float32)
        total += jnp.sum(hidden * back, axis=1, keepdims=True)
        scaled = prob * back
        grads_ref[:, c * part : (c + 1) * part] = (
            scaled * up * squash * (1.0 + gate * (1.0 - squash))
        ).astype(jnp.bfloat16)
        grads_ref[:, FFW + c * part : FFW + (c + 1) * part] = (scaled * silu).astype(jnp.bfloat16)
    grad_probs_ref[...] = jnp.broadcast_to(total, square).T[:1].astype(jnp.bfloat16)


def onehot(index, rows):
    return (jnp.arange(rows, dtype=jnp.int32)[:, None] == index[None, :]).astype(jnp.bfloat16)


def body(cotangent, gate_up, route_probs, routes, down_weight):
    tokens = cotangent.shape[0]

    own = down_weight[0]
    line = lax.all_to_all(
        pl.pallas_call(
            spread,
            out_shape=jax.ShapeDtypeStruct((RING,) + own.shape, jnp.bfloat16),
            in_specs=[pl.BlockSpec(memory_space=pltpu.VMEM)],
            out_specs=pl.BlockSpec(memory_space=pltpu.VMEM),
        )(own),
        TORUS,
        split_axis=0,
        concat_axis=0,
        axis_index_groups=first_groups(),
        tiled=True,
    )

    flat_routes = routes.reshape(tokens)
    member = (flat_routes[:, None] == jnp.arange(EXPERTS, dtype=jnp.int32)[None, :]).astype(jnp.int32)
    rank = jnp.sum(jnp.cumsum(member, axis=0) * member, axis=1) - 1
    first = flat_routes * (2 * CAP) + rank
    both = jnp.concatenate([first, first + CAP])
    placing = onehot(both, EXPERTS * 2 * CAP)
    quarters = [cotangent[:, i * QUART : (i + 1) * QUART] for i in range(4)]
    sent = jnp.stack(
        [
            jnp.dot(
                placing,
                jnp.concatenate([quarters[2 * h], quarters[2 * h + 1]], axis=0),
                preferred_element_type=jnp.float32,
            ).astype(jnp.bfloat16)
            for h in range(2)
        ]
    ).reshape(PEERS, 2 * CAP, QUART)
    line, sent = lax.optimization_barrier((line, sent))
    ahead = lax.ppermute(line, TORUS, second_shift(-3))
    behind = lax.ppermute(line, TORUS, second_shift(3))
    passed = jax.ShapeDtypeStruct((2 * RING + HALF_RING,) + own.shape, jnp.bfloat16)
    up, down = pl.pallas_call(
        join,
        out_shape=(passed, passed),
        in_specs=[pl.BlockSpec(memory_space=pltpu.VMEM)] * 3,
        out_specs=(pl.BlockSpec(memory_space=pltpu.VMEM),) * 2,
        compiler_params=pltpu.CompilerParams(vmem_limit_bytes=16 * 2**20),
        cost_estimate=pl.CostEstimate(flops=2 * 10**11, bytes_accessed=4 * 10**6, transcendentals=0),
    )(line, ahead, behind)
    parts = [line, ahead, behind, lax.ppermute(up, TORUS, second_shift(1)), lax.ppermute(down, TORUS, second_shift(-1))]
    got = lax.all_to_all(sent, SHARE, split_axis=0, concat_axis=0, tiled=True)

    back = pl.pallas_call(
        product,
        out_shape=jax.ShapeDtypeStruct((COUNT, FFW // 2), jnp.bfloat16),
        in_specs=[pl.BlockSpec(memory_space=pl.ANY)] + [pl.BlockSpec(memory_space=pltpu.VMEM)] * ARRAYS,
        out_specs=pl.BlockSpec(memory_space=pltpu.VMEM),
        scratch_shapes=[
            pltpu.VMEM((RING * RING,) + own.shape, jnp.bfloat16),
            pltpu.VMEM((COUNT, QUART), jnp.bfloat16),
            pltpu.VMEM((COUNT, QUART), jnp.bfloat16),
            pltpu.SemaphoreType.DMA,
        ],
        compiler_params=pltpu.CompilerParams(vmem_limit_bytes=20 * 2**20),
        cost_estimate=pl.CostEstimate(flops=2 * 10**9, bytes_accessed=10**7, transcendentals=0),
    )(got.reshape(COUNT, QUART), *parts)
    came = lax.all_to_all(
        back.reshape(PEERS, 2 * CAP, FFW // 2), SHARE, split_axis=0, concat_axis=0, tiled=True
    ).reshape(COUNT, FFW // 2)

    grads, grad_probs = pl.pallas_call(
        finish,
        out_shape=(
            jax.ShapeDtypeStruct((tokens, 2 * FFW), jnp.bfloat16),
            jax.ShapeDtypeStruct((1, tokens), jnp.bfloat16),
        ),
        in_specs=[pl.BlockSpec(memory_space=pltpu.VMEM)] * 4,
        out_specs=(pl.BlockSpec(memory_space=pltpu.VMEM),) * 2,
        compiler_params=pltpu.CompilerParams(vmem_limit_bytes=20 * 2**20),
        cost_estimate=pl.CostEstimate(flops=2 * 10**8, bytes_accessed=2 * 10**6, transcendentals=10**5),
    )(came, gate_up.reshape(tokens, 2 * FFW), route_probs.reshape(1, tokens), first.reshape(1, tokens))
    return grads.reshape(tokens, 1, 2 * FFW), grad_probs.reshape(tokens, 1)


def solution(mesh):
    named = Mesh(mesh.devices.reshape(2, 8, 8, 4, 2), AXES)
    return jax.shard_map(
        body,
        mesh=named,
        in_specs=(
            P(AXES, None),
            P(AXES, None, None),
            P(AXES, None),
            P(AXES, None),
            P(("xh", "core"), ("xl", "y", "z"), None),
        ),
        out_specs=(P(AXES, None, None), P(AXES, None)),
        check_vma=False,
    )
```
